32 devices in a mesh: row: 4 (over y, x), grp: 4 (over z), col: 2 (over core).
Axes of the slice: x: 2, y: 2, z: 4, core: 2. Of those that a mesh axis runs over, the one named last changes fastest.
Arguments:
- state: float32 [64, 128, 256], P('row', ('grp', 'col')), may hold values from -6 to 6
- rate: float32 [64, 128], P('row', ('grp', 'col')), may hold values from 0.02 to 0.24
- cotangent: bfloat16 [64, 128, 256], P('row', ('grp', 'col')), may hold values from -6 to 6
- dest: int32 [4, 8, 256, 1], P('row', ('grp', 'col')), may hold values from 0 to 3; in each aligned block of 256 rows (0 to 255, 256 to 511, ..., all dimensions but the last counted through in order) at most 128 rows name the same one
- w_in: bfloat16 [4, 256, 1024], P('grp'), may hold values from -0.375 to 0.375
- w_out: bfloat16 [4, 256, 1024], P('grp'), may hold values from -0.1875 to 0.1875
Outputs:
- new_state: float32 [64, 128, 256], P('row', ('grp', 'col'))
- column_adjoint: bfloat16 [64, 128, 256], P('row', ('grp', 'col'))
- weight_grads: float32 [4, 4096, 128], P('grp', ('row', 'col'))
The draws below stay inside these ranges and needn't reach their ends.
Inputs may be any that keep to these rules, and one draw needn't show every extreme that they name: `dest`: within one block no owner receives more than 128 columns, and some owner receives exactly 128 in some block.
All inputs are finite; a program needn't handle non-finite values.
Results may differ from the reference program's by a relative error of at most 0.0053.
Values may be sent and summed in bfloat16 or wider, within the bound.
No kernel may reach another device: no remote copies, remote signals or barrier semaphores. Data moves between devices by JAX's collectives and lax.ppermute only.
A program may use at most 64 MiB of HBM per device.

```python
import math
import jax
import jax.numpy as jnp
import numpy as np
from jax import lax

FIELDS = 8
LEV = 32
HID = 1024
BX = 16
BY = 16
STEPS = 4
CAP = 128
EXPERTS = 4
NX = 64
NY = 128
FLAT = 4096
N_ROW = 4
N_GRP = 4
N_COL = 2


def levels(stream_key, shape, cuts, least, largest):
    loudness, own = 1.0, jax.random.fold_in(stream_key, 6)
    for dim, parts in cuts:
        draws = jnp.exp(jax.random.uniform(jax.random.fold_in(own, dim), (parts,), jnp.float32, least / len(cuts), largest / len(cuts)))
        loudness = loudness * jnp.repeat(draws, shape[dim] // parts).reshape([-1 if axis == dim else 1 for axis in range(len(shape))])
    return loudness


def assign_block(key, own, number, rows, count, top, most, slope):
    ranking = jax.random.permutation(key, count)
    heavy_load, common = shares(count, rows * top, most, slope, True), shares(count, rows * top, most, slope, False)
    places = jnp.arange(count)

    def named(lengths, offset_by):
        used = int((lengths > 0).sum())
        fixed = max(1, used // 4)
        moved = fixed + (places - fixed + offset_by * (used - fixed)) % max(1, count - fixed)
        return jnp.zeros((count,), jnp.int32).at[ranking[jnp.where(places < fixed, places, moved)]].set(jnp.asarray(lengths, jnp.int32))

    lengths = jnp.where(number % 4 == 0, named(heavy_load, number // 4), named(common, number - number // 4 - 1))
    mixed = jax.random.permutation(jax.random.fold_in(own, 3), count)
    source_of, sink = mixed[0:count // 2 * 2:2], mixed[1:count // 2 * 2:2]
    margin = jnp.minimum(lengths[source_of] - 1, most - lengths[sink]) // 2
    margin = jnp.where((source_of == ranking[0]) | (sink == ranking[0]) | (lengths[sink] == 0), 0, jnp.maximum(margin, 0))
    moved = jax.random.randint(jax.random.fold_in(own, 4), (count // 2,), 0, 1 << 20) % (margin + 1)
    lengths = lengths.at[source_of].add(-moved).at[sink].add(moved)
    members = jnp.searchsorted(jnp.cumsum(lengths), jnp.arange(rows * top), side="right").astype(jnp.int32)
    table = members.reshape(top, rows).T
    table = table[jax.random.permutation(jax.random.fold_in(own, 1), rows)]
    offset_by = jax.random.randint(jax.random.fold_in(own, 2), (rows, 1), 0, top)
    return jnp.take_along_axis(table, (jnp.arange(top)[None, :] + offset_by) % top, axis=1)


def shares(count, total, most, skew, full):
    weights = [(1 << 20) // math.isqrt(rank ** skew) + 1 for rank in range(1, count + 1)]
    largest = most if full else min(most, max(-(-total // count), total * weights[0] // sum(weights)))
    least = 1 if total - largest >= count - 1 else 0
    holding, rest = [largest] + [least] * (count - 1), total - largest - least * (count - 1)
    while rest > 0:
        free = [i for i in range(1, count) if holding[i] < largest] or [i for i in range(1, count) if holding[i] < most]
        whole, remaining = sum([weights[i] for i in free]), rest
        for i in free:
            addition = min(most - holding[i], max(1, remaining * weights[i] // whole), rest)
            holding[i] = holding[i] + addition
            rest = rest - addition
    return np.array(holding)


def gaussian(stream_key, shape, spread, reach, shards=(), kind=jnp.bfloat16):
    array = jax.random.normal(stream_key, shape, jnp.float32) * spread
    if len(shards) > 0:
        array = levels(stream_key, shape, shards, -0.22, 0.18) * array
    return jnp.clip(array, min=-reach, max=reach).astype(kind)


def setup_inputs(seed: int = 0) -> dict:
    keys = jax.random.split(jax.random.key(seed), 7)
    state = gaussian(keys[0], (NX, NY, FIELDS * LEV), 1.0, 6.0, ((0, 4), (1, 8)), jnp.float32)
    rate = jnp.clip(jnp.exp(math.log(0.24) - 2.4849066 * jax.random.uniform(keys[1], (NX, NY), jnp.float32) ** levels(keys[1], (NX, NY), ((0, 4), (1, 8)), -0.2, 0.2)), 0.02, 0.24)
    cotangent = gaussian(keys[2], (NX, NY, FIELDS * LEV), 1.0, 6.0, ((0, 4), (1, 8)))
    dest_keys = jax.random.split(jax.random.fold_in(keys[3], 1), N_ROW * (N_GRP * N_COL) * (BX * BY) // (BX * BY))
    dest_turns = jax.random.permutation(jax.random.fold_in(keys[3], 3), N_ROW * (N_GRP * N_COL) * (BX * BY) // (BX * BY))
    dest = jax.vmap(lambda own, number: assign_block(jax.random.fold_in(keys[3], 2), own, number, BX * BY, N_GRP, 1, 2 * BX * BY // N_GRP, 2))(dest_keys, dest_turns).reshape((N_ROW, N_GRP * N_COL, BX * BY, 1))
    w_in = gaussian(keys[4], (EXPERTS, FIELDS * LEV, HID), (FIELDS * LEV) ** -0.5, 0.375, ((0, 4),))
    w_out = gaussian(keys[5], (EXPERTS, FIELDS * LEV, HID), HID ** -0.5, 0.1875, ((0, 4),))
    return dict(state=state, rate=rate, cotangent=cotangent, dest=dest, w_in=w_in, w_out=w_out)


def silu_slope(value):
    logistic = jax.nn.sigmoid(value)
    return logistic * (1.0 + value * (1.0 - logistic))


def reference(state, rate, cotangent, dest, w_in, w_out):
    feats = FIELDS * LEV
    field = state
    for step in range(STEPS):
        beside = jnp.roll(field, 1, 0) + jnp.roll(field, -1, 0) + jnp.roll(field, 1, 1) + jnp.roll(field, -1, 1)
        field = field + rate[:, :, None] * (beside - 4.0 * field)

    def to_groups(grid):
        shaped = grid.reshape(N_ROW, BX, N_GRP, N_COL, BY, feats)
        shaped = shaped.transpose(0, 3, 2, 1, 4, 5)
        return shaped.reshape(N_ROW * N_COL, N_GRP, BX * BY, feats)

    def from_groups(groups):
        shaped = groups.reshape(N_ROW, N_COL, N_GRP, BX, BY, feats)
        shaped = shaped.transpose(0, 3, 2, 1, 4, 5)
        return shaped.reshape(N_ROW * BX, N_GRP * N_COL * BY, feats)

    columns = to_groups(state.astype(jnp.bfloat16))
    cotans = to_groups(cotangent)
    routes = dest.reshape(N_ROW, N_GRP, N_COL, BX * BY).transpose(0, 2, 1, 3).reshape(N_ROW * N_COL, N_GRP, BX * BY)
    onehot = (routes[..., None] == jnp.arange(N_GRP, dtype=jnp.int32)).astype(jnp.int32)
    ranks = jnp.cumsum(onehot, axis=2) - 1
    slots = jnp.sum(ranks * onehot, axis=-1)
    places = (routes * CAP + slots).astype(jnp.int32)
    w_in32 = w_in.astype(jnp.float32)
    w_out32 = w_out.astype(jnp.float32)

    def pack_one(rows, where):
        return jnp.zeros((N_GRP * CAP, feats), rows.dtype).at[where].set(rows)

    def group_step(carry, pieces):
        group_cols, group_cots, group_places = pieces
        packed_cols = jax.vmap(pack_one)(group_cols, group_places)
        packed_cots = jax.vmap(pack_one)(group_cots, group_places)
        owner_cols = packed_cols.reshape(N_GRP, N_GRP, CAP, feats).transpose(1, 0, 2, 3).reshape(N_GRP, N_GRP * CAP, feats)
        owner_cots = packed_cots.reshape(N_GRP, N_GRP, CAP, feats).transpose(1, 0, 2, 3).reshape(N_GRP, N_GRP * CAP, feats)
        cols32 = owner_cols.astype(jnp.float32)
        pre = jnp.einsum("erf,efh->erh", cols32, w_in32)
        act = jax.nn.silu(pre).astype(jnp.bfloat16)
        act32 = act.astype(jnp.float32)
        tend = jnp.einsum("erh,efh->erf", act32, w_out32).astype(jnp.bfloat16)
        dtend = (0.5 * owner_cots.astype(jnp.float32)).astype(jnp.bfloat16)
        dtend32 = dtend.astype(jnp.float32)
        dact = jnp.einsum("erf,efh->erh", dtend32, w_out32)
        dpre = (dact * silu_slope(pre)).astype(jnp.bfloat16)
        dpre32 = dpre.astype(jnp.float32)
        adjoint = jnp.einsum("erh,efh->erf", dpre32, w_in32).astype(jnp.bfloat16)
        grad_in = jnp.einsum("erf,erh->efh", cols32, dpre32)
        grad_out = jnp.einsum("erf,erh->efh", dtend32, act32)
        carry = carry + jnp.stack([grad_in, grad_out], axis=1)

        def unpack(owner_rows):
            by_source = owner_rows.reshape(N_GRP, N_GRP, CAP, feats).transpose(1, 0, 2, 3).reshape(N_GRP, N_GRP * CAP, feats)
            return jax.vmap(lambda rows, where: jnp.take(rows, where, axis=0))(by_source, group_places)

        return carry, (unpack(tend), unpack(adjoint))

    start = jnp.zeros((N_GRP, 2, feats, HID), jnp.float32)
    grads, (tends, adjoints) = lax.scan(group_step, start, (columns, cotans, places))
    tendency = from_groups(tends)
    column_adjoint = from_groups(adjoints)
    new_state = field + 0.5 * tendency.astype(jnp.float32)
    weight_grads = grads.reshape(N_GRP, FLAT, 128)
    return new_state, column_adjoint, weight_grads
```

```python
import functools

import jax
import jax.numpy as jnp
from jax import lax
from jax.experimental import pallas as pl
from jax.experimental.pallas import tpu as pltpu
from jax.sharding import PartitionSpec as P

STEPS = 4
BF16 = jnp.bfloat16
F32 = jnp.float32
VMEM = pl.BlockSpec(memory_space=pltpu.VMEM)
SMEM = pl.BlockSpec(memory_space=pltpu.SMEM)


def call(kernel, ins, outs, scratch=(), flops=0, vmem=24 << 20):
    moved = sum(x.size * x.dtype.itemsize for x in ins) + sum(
        o.size * o.dtype.itemsize for o in outs
    )
    specs = [SMEM if x.ndim == 1 else VMEM for x in ins]
    return pl.pallas_call(
        kernel,
        out_shape=list(outs),
        in_specs=specs,
        out_specs=[VMEM] * len(outs),
        scratch_shapes=list(scratch),
        compiler_params=pltpu.CompilerParams(vmem_limit_bytes=vmem),
        cost_estimate=pl.CostEstimate(flops=flops, bytes_accessed=moved, transcendentals=0),
    )(*ins)


def shape(dims, dtype):
    return jax.ShapeDtypeStruct(dims, dtype)


def nt(a, b):
    return lax.dot_general(a, b, (((1,), (1,)), ((), ())), preferred_element_type=F32)


def nn(a, b):
    return jnp.dot(a, b, preferred_element_type=F32)


def pack_kernel(owners, cap, wide, high, where, state, cot, dest, rate, *outs):
    chunks, up, down = outs[:owners], outs[owners], outs[owners + 1]
    count, feats = state.shape
    named = lax.broadcasted_iota(jnp.int32, (max(8, owners), count), 0) == dest[...]
    earlier = lax.broadcasted_iota(jnp.int32, (count, count), 0) < lax.broadcasted_iota(
        jnp.int32, (count, count), 1
    )
    ranks = nn(named.astype(F32).astype(BF16), earlier.astype(F32).astype(BF16))
    slot = jnp.sum(jnp.where(named, ranks, 0.0), axis=0, keepdims=True).astype(jnp.int32)
    place = (dest[...] ^ where[0]) * cap + slot
    cols = state[...].astype(BF16)
    cots = cot[...]
    for k in range(owners):
        rows = lax.broadcasted_iota(jnp.int32, (cap, count), 0) + k * cap
        placing = (rows == place).astype(F32).astype(BF16)
        chunks[k][:, :feats] = nn(placing, cols).astype(BF16)
        chunks[k][:, feats:] = nn(placing, cots).astype(BF16)
    strip = STEPS * wide
    for out, start in ((up, 0), (down, count - strip)):
        out[:, :feats] = state[start : start + strip].astype(BF16)
        out[:, feats:] = jnp.broadcast_to(rate[start : start + strip], (strip, 128)).astype(BF16)


def edge_kernel(wide, high, state, rate, above, below, dest, where, left, right, places):
    feats = state.shape[1]
    span = high + 2 * STEPS
    half = span // 2
    low = lax.broadcasted_iota(jnp.int32, (8, feats + 128), 0) < STEPS
    tiles = []
    for r in range(span):
        if r < high:
            first = [
                jnp.concatenate(
                    [
                        state[r * wide + c : r * wide + c + 8],
                        jnp.broadcast_to(rate[r * wide + c : r * wide + c + 8], (8, 128)),
                    ],
                    axis=1,
                )
                for c in (0, wide - 8)
            ]
        else:
            ref, at = (below, r - high) if r < high + STEPS else (above, r - high - STEPS)
            both = ref[at * wide : (at + 1) * wide].astype(F32)
            first = [both[:8], both[wide - 8 :]]
        tiles.append(jnp.where(low, first[0], first[1]))
    lefts, rights = [], []
    for i in range(half):
        turned = pltpu.roll(tiles[i + half], STEPS, 0)
        lefts.append(jnp.where(low, tiles[i], turned))
        rights.append(jnp.where(low, turned, tiles[i]))
    for i in range(0, half, 2):
        left[i * 8 : i * 8 + 16] = jnp.concatenate(lefts[i : i + 2], axis=0).astype(BF16)
        right[i * 8 : i * 8 + 16] = jnp.concatenate(rights[i : i + 2], axis=0).astype(BF16)
    count = state.shape[0]
    lanes = 128
    named = lax.broadcasted_iota(jnp.int32, (count, lanes), 1) == dest[...]
    earlier = lax.broadcasted_iota(jnp.int32, (count, count), 1) < lax.broadcasted_iota(
        jnp.int32, (count, count), 0
    )
    ranks = nn(earlier.astype(F32).astype(BF16), named.astype(F32).astype(BF16))
    slot = jnp.sum(jnp.where(named, ranks, 0.0), axis=1, keepdims=True).astype(jnp.int32)
    owners_cap = places.shape[1]
    place = (dest[...] ^ where[0]) * where[1] + slot
    hits = lax.broadcasted_iota(jnp.int32, (count, owners_cap), 1) == place
    places[...] = hits.astype(F32).astype(BF16)


def flow_kernel(wide, high, state, rate, above, below, lefts, rights, out, grid, rates):
    feats = state.shape[1]
    span, across = high + 2 * STEPS, wide + 2 * STEPS
    half = span // 2
    low = lax.broadcasted_iota(jnp.int32, (8, feats + 128), 0) < STEPS
    for i in range(half):
        from_right = rights[i * 8 : i * 8 + 8].astype(F32)
        from_left = lefts[i * 8 : i * 8 + 8].astype(F32)
        near = jnp.where(low, from_right, from_left)
        far = pltpu.roll(jnp.where(low, from_left, from_right), STEPS, 0)
        for r, tile in ((i, near), (i + half, far)):
            grid[0, r, wide:] = tile[:, :feats]
            rates[r, wide:] = tile[:, feats:]
    for r in range(high):
        grid[0, r, :wide] = state[r * wide : (r + 1) * wide]
        rates[r, :wide] = jnp.broadcast_to(rate[r * wide : (r + 1) * wide], (wide, 128))
    for at in range(STEPS):
        for ref, start in ((below, high), (above, high + STEPS)):
            strip = ref[at * wide : (at + 1) * wide].astype(F32)
            grid[0, start + at, :wide] = strip[:, :feats]
            rates[start + at, :wide] = strip[:, feats:]
    for step in range(STEPS):
        now, later = step % 2, (step + 1) % 2
        margin = STEPS - 1 - step
        for r in [r % span for r in range(-margin, high + margin)]:
            here = grid[now, r]
            beside = (
                grid[now, (r - 1) % span]
                + grid[now, (r + 1) % span]
                + pltpu.roll(here, 1, 0)
                + pltpu.roll(here, across - 1, 0)
            )
            amount = rates[r]
            amount = jnp.concatenate([amount] * (feats // 128), axis=1)
            here = here + amount * (beside - 4.0 * here)
            if step == STEPS - 1:
                out[r * wide : (r + 1) * wide] = here[:wide]
            else:
                grid[later, r] = here


def physics_kernel(chunk, w_in, w_out, back, act_out, dpre_out):
    feats, hidden = w_in.shape
    cols = chunk[:, :feats]
    dtend = (0.5 * chunk[:, feats:].astype(F32)).astype(BF16)
    tend = adjoint = None
    piece = 256
    for h in range(0, hidden, piece):
        win, wout = w_in[:, h : h + piece], w_out[:, h : h + piece]
        pre = nn(cols, win)
        dact = nn(dtend, wout)
        sigma = 1.0 / (1.0 + jnp.exp(-pre))
        act = (pre * sigma).astype(BF16)
        dpre = (dact * (sigma * (1.0 + pre * (1.0 - sigma)))).astype(BF16)
        act_out[:, h : h + piece] = act
        dpre_out[:, h : h + piece] = dpre
        tend_h, adj_h = nt(act, wout), nt(dpre, win)
        tend = tend_h if tend is None else tend + tend_h
        adjoint = adj_h if adjoint is None else adjoint + adj_h
    back[:, :feats] = tend.astype(BF16)
    back[:, feats:] = adjoint.astype(BF16)


def grads_of(chunks, acts, dpres, h, piece, feats):
    dpre = jnp.concatenate([d[:, h : h + piece] for d in dpres], axis=0)
    act = jnp.concatenate([a[:, h : h + piece] for a in acts], axis=0)
    return dpre, act


def grads_kernel(owners, where, *refs):
    chunks, acts, dpres = refs[:owners], refs[owners : 2 * owners], refs[2 * owners : 3 * owners]
    keep, send = refs[3 * owners :]
    feats = chunks[0].shape[1] // 2
    hidden = acts[0].shape[1]
    block = keep.shape[2]
    cols = jnp.concatenate([c[:, :feats] for c in chunks], axis=0).T
    cots = jnp.concatenate([c[:, feats:] for c in chunks], axis=0)
    dtend = (0.5 * cots.astype(F32)).astype(BF16).T
    core = where[2]
    piece = 256
    for h in range(0, hidden, piece):
        dpre, act = grads_of(chunks, acts, dpres, h, piece, feats)
        for which, total in ((0, nn(cols, dpre)), (1, nn(dtend, act))):
            for x in range(2):
                one = total[2 * x * block : (2 * x + 1) * block]
                two = total[(2 * x + 1) * block : (2 * x + 2) * block]
                keep[which, x, :, h : h + piece] = jnp.where(core == 0, one, two)
                send[which, x, :, h : h + piece] = jnp.where(core == 0, two, one).astype(BF16)


def whole_grads_kernel(owners, *refs):
    chunks, acts, dpres = refs[:owners], refs[owners : 2 * owners], refs[2 * owners : 3 * owners]
    out = refs[3 * owners]
    feats = chunks[0].shape[1] // 2
    cols = jnp.concatenate([c[:, :feats] for c in chunks], axis=0).T
    cots = jnp.concatenate([c[:, feats:] for c in chunks], axis=0)
    dtend = (0.5 * cots.astype(F32)).astype(BF16).T
    piece = 256
    for h in range(0, acts[0].shape[1], piece):
        dpre, act = grads_of(chunks, acts, dpres, h, piece, feats)
        out[:feats, h : h + piece] = nn(cols, dpre)
        out[feats:, h : h + piece] = nn(dtend, act)


def share_kernel(where, keep, got, mine, *sends):
    y, x = where[3], where[4]
    mine[...] = keep[y, x] + got[y, x].astype(F32)
    for send, (dy, dx) in zip(sends, ((0, 1), (1, 0), (1, 1))):
        send[...] = (keep[y ^ dy, x ^ dx] + got[y ^ dy, x ^ dx].astype(F32)).astype(BF16)


def gather_kernel(mine, one, two, three, out):
    rows, hidden = mine.shape
    for j in range(hidden // 128):
        at = slice(j * 128, (j + 1) * 128)
        total = mine[:, at] + one[:, at].astype(F32) + (two[:, at].astype(F32) + three[:, at].astype(F32))
        out[pl.ds(j, rows, stride=hidden // 128), :] = total


def finish_kernel(owners, field, places, *refs):
    backs, new_state, column_adjoint = refs[:owners], refs[owners], refs[owners + 1]
    feats = field.shape[1]
    cap = backs[0].shape[0]
    rows = nn(places[...], jnp.concatenate([b[...] for b in backs], axis=0))
    new_state[...] = field[...] + 0.5 * rows[:, :feats]
    column_adjoint[...] = rows[:, feats:].astype(BF16)


def ring(axis, step):
    count = lax.axis_size(axis)
    return [(i, (i + step) % count) for i in range(count)]


def swap(axis, bit):
    return [(i, i ^ bit) for i in range(lax.axis_size(axis))]


def local(state, rate, cotangent, dest, w_in, w_out):
    high, wide, feats = state.shape
    count = high * wide
    owners = lax.axis_size("grp")
    cap = 2 * count // owners
    hidden = w_in.shape[2]
    grp, row, core = lax.axis_index("grp"), lax.axis_index("row"), lax.axis_index("col")
    where = jnp.stack([grp, jnp.int32(cap), core, row // 2, row % 2]).astype(jnp.int32)
    flat_state = state.reshape(count, feats)
    flat_cot = cotangent.reshape(count, feats)
    rate_col = rate.reshape(count, 1)
    dest_col = dest.reshape(count, 1)
    weight_in, weight_out = w_in[0], w_out[0]

    strip = shape((STEPS * wide, feats + 128), BF16)
    *chunks, up, down = call(
        functools.partial(pack_kernel, owners, cap, wide, high),
        [where, flat_state, flat_cot, dest.reshape(1, count), rate_col],
        [shape((cap, 2 * feats), BF16)] * owners + [strip, strip],
        flops=2 * owners * cap * count * 2 * feats,
    )
    got = [chunks[0]] + [None] * (owners - 1)
    for k in range(owners - 1, 0, -1):
        got[k] = lax.ppermute(chunks[k], "grp", swap("grp", k))
    above = lax.ppermute(down, "row", ring("row", 1))
    below = lax.ppermute(up, "row", ring("row", -1))

    backs, acts, dpres = [None] * owners, [None] * owners, [None] * owners

    def physics(k):
        backs[k], acts[k], dpres[k] = call(
            physics_kernel,
            [got[k], weight_in, weight_out],
            [
                shape((cap, 2 * feats), BF16),
                shape((cap, hidden), BF16),
                shape((cap, hidden), BF16),
            ],
            flops=8 * cap * feats * hidden,
        )
        if k > 0:
            backs[k] = lax.ppermute(backs[k], "grp", swap("grp", k))

    physics(0)
    side = shape(((high + 2 * STEPS) * STEPS, feats + 128), BF16)
    to_left, to_right, places = call(
        functools.partial(edge_kernel, wide, high),
        [flat_state, rate_col, above, below, dest_col, where],
        [side, side, shape((count, owners * cap), BF16)],
        flops=2 * count * count * 128,
    )
    from_left = lax.ppermute(to_right, ("grp", "col"), ring(("grp", "col"), 1))
    from_right = lax.ppermute(to_left, ("grp", "col"), ring(("grp", "col"), -1))
    for k in range(1, owners):
        physics(k)
    (field,) = call(
        functools.partial(flow_kernel, wide, high),
        [flat_state, rate_col, above, below, from_left, from_right],
        [shape((count, feats), F32)],
        [
            pltpu.VMEM((2, high + 2 * STEPS, wide + 2 * STEPS, feats), F32),
            pltpu.VMEM((high + 2 * STEPS, wide + 2 * STEPS, 128), F32),
        ],
        flops=40 * count * feats,
    )

    parts = lax.axis_size("row") * lax.axis_size("col")
    block = 2 * feats // parts
    grad_flops = 4 * owners * cap * feats * hidden
    if lax.axis_size("row") == 4 and lax.axis_size("col") == 2:
        keep, send = call(
            functools.partial(grads_kernel, owners),
            [where, *got, *acts, *dpres],
            [shape((2, 2, block, hidden), F32), shape((2, 2, block, hidden), BF16)],
            flops=grad_flops,
        )
        arrived = lax.ppermute(send, "col", swap("col", 1))
        mine, *shares = call(
            share_kernel,
            [where, keep, arrived],
            [shape((block, hidden), F32)] + [shape((block, hidden), BF16)] * 3,
        )
        shares = [lax.ppermute(s, "row", swap("row", bit + 1)) for bit, s in enumerate(shares)]
        (summed,) = call(
            gather_kernel, [mine, *shares], [shape((block * hidden // 128, 128), F32)]
        )
    else:
        (flat,) = call(
            functools.partial(whole_grads_kernel, owners),
            [*got, *acts, *dpres],
            [shape((2 * feats, hidden), F32)],
            flops=grad_flops,
        )
        summed = lax.psum_scatter(
            flat.reshape(-1, 128), ("row", "col"), scatter_dimension=0, tiled=True
        )
    new_state, column_adjoint = call(
        functools.partial(finish_kernel, owners),
        [field, places, *backs],
        [shape((count, feats), F32), shape((count, feats), BF16)],
        flops=4 * count * owners * cap * feats,
    )
    return (
        new_state.reshape(state.shape),
        column_adjoint.reshape(state.shape),
        summed[None],
    )


def solution(mesh):
    in_specs = (
        P("row", ("grp", "col"), None),
        P("row", ("grp", "col")),
        P("row", ("grp", "col"), None),
        P("row", ("grp", "col"), None, None),
        P("grp", None, None),
        P("grp", None, None),
    )
    out_specs = (
        P("row", ("grp", "col"), None),
        P("row", ("grp", "col"), None),
        P("grp", ("row", "col"), None),
    )
    return jax.shard_map(local, mesh=mesh, in_specs=in_specs, out_specs=out_specs, check_vma=False)
```

```python
import functools

import jax
import jax.numpy as jnp
from jax import lax
from jax.experimental import pallas as pl
from jax.experimental.pallas import tpu as pltpu
from jax.sharding import PartitionSpec as P

STEPS = 4
BF16 = jnp.bfloat16
F32 = jnp.float32
VMEM = pl.BlockSpec(memory_space=pltpu.VMEM)
HBM = pl.BlockSpec(memory_space=pltpu.HBM)
ANY = pl.BlockSpec(memory_space=pl.ANY)


def call(kernel, ins, outs, scratch=(), after=(), far=(), vmem=24 << 20):
    specs = [HBM if n in far else VMEM for n in range(len(ins))]
    count = len(ins)

    def body(*refs):
        kernel(*refs[:count], *refs[count + len(after) :])

    return pl.pallas_call(
        body,
        out_shape=list(outs),
        in_specs=specs + [ANY] * len(after),
        out_specs=[VMEM] * len(outs),
        scratch_shapes=list(scratch),
        compiler_params=pltpu.CompilerParams(vmem_limit_bytes=vmem),
    )(*ins, *after)


def shape(dims, dtype):
    return jax.ShapeDtypeStruct(dims, dtype)


def nt(a, b):
    return lax.dot_general(a, b, (((1,), (1,)), ((), ())), preferred_element_type=F32)


def nn(a, b):
    return jnp.dot(a, b, preferred_element_type=F32)


def pack_kernel(owners, cap, wide, high, *refs):
    far, near, sems = refs[:4], refs[-5:-1], refs[-1]
    chunks, inner, outer, rate_cols, places = refs[4 : owners + 4], *refs[owners + 4 : -5]
    copies = [pltpu.make_async_copy(a, b, sems.at[n]) for n, (a, b) in enumerate(zip(far, near))]
    for copy in copies:
        copy.start()
    dest, rate, state, cot = near
    count, feats = state.shape
    copies[0].wait()
    named = lax.broadcasted_iota(jnp.int32, (max(8, owners), count), 0) == dest[...]
    earlier = lax.broadcasted_iota(jnp.int32, (count, count), 0) < lax.broadcasted_iota(
        jnp.int32, (count, count), 1
    )
    ranks = nn(named.astype(F32).astype(BF16), earlier.astype(F32).astype(BF16))
    slot = jnp.sum(jnp.where(named, ranks, 0.0), axis=0, keepdims=True).astype(jnp.int32)
    apart = dest[...] ^ lax.axis_index("grp")
    place = jnp.where(lax.axis_index("col") == 0, apart, (owners - apart) & (owners - 1)) * cap + slot
    places[...] = place
    for copy in copies[1:]:
        copy.wait()
    turned = rate[...].T
    for r in range(high):
        rate_cols[r * wide : (r + 1) * wide] = turned[:, r : r + 1]
    cols = state[...].astype(BF16)
    cots = cot[...]
    for k in range(owners):
        rows = lax.broadcasted_iota(jnp.int32, (cap, count), 0) + k * cap
        placing = (rows == place).astype(F32).astype(BF16)
        chunks[k][:, :feats] = nn(placing, cols).astype(BF16)
        chunks[k][:, feats:] = nn(placing, cots).astype(BF16)
    strip = STEPS * wide
    odd = lax.rem(lax.axis_index("row"), 2)
    for out, top in ((inner, odd), (outer, 1 - odd)):
        start = pl.multiple_of((1 - top) * (count - strip), strip)
        out[:, :feats] = state[pl.ds(start, strip)].astype(BF16)
        out[:, feats:] = jnp.broadcast_to(rate_cols[pl.ds(start, strip)], (strip, 128)).astype(BF16)


def edge_kernel(wide, high, state, rate, near, far, place_row, inner, outer, places):
    feats = state.shape[1]
    span = high + 2 * STEPS
    half = span // 2
    odd, core = lax.rem(lax.axis_index("row"), 2), lax.axis_index("col")
    low = lax.broadcasted_iota(jnp.int32, (8, feats + 128), 0) < STEPS
    tiles = []
    for r in range(span):
        if r < high:
            first = [
                jnp.concatenate(
                    [
                        state[r * wide + c : r * wide + c + 8],
                        jnp.broadcast_to(rate[r * wide + c : r * wide + c + 8], (8, 128)),
                    ],
                    axis=1,
                )
                for c in (0, wide - 8)
            ]
        else:
            at = slice((r - high) % STEPS * wide, ((r - high) % STEPS + 1) * wide)
            is_near = (odd == 0) if r < high + STEPS else (odd == 1)
            both = jnp.where(is_near, near[at].astype(F32), far[at].astype(F32))
            first = [both[:8], both[wide - 8 :]]
        tiles.append(jnp.where(low, first[0], first[1]))
    lefts, rights = [], []
    for i in range(half):
        turned = pltpu.roll(tiles[i + half], STEPS, 0)
        lefts.append(jnp.where(low, tiles[i], turned))
        rights.append(jnp.where(low, turned, tiles[i]))
    for i in range(0, half, 2):
        one = jnp.concatenate(lefts[i : i + 2], axis=0)
        two = jnp.concatenate(rights[i : i + 2], axis=0)
        inner[i * 8 : i * 8 + 16] = jnp.where(core == 0, two, one).astype(BF16)
        outer[i * 8 : i * 8 + 16] = jnp.where(core == 0, one, two).astype(BF16)
    count = state.shape[0]
    same = lax.broadcasted_iota(jnp.int32, (count, count), 0) == lax.broadcasted_iota(
        jnp.int32, (count, count), 1
    )
    place = jnp.sum(jnp.where(same, place_row[...], 0).astype(F32), axis=1, keepdims=True)
    hits = lax.broadcasted_iota(jnp.int32, places.shape, 1) == place.astype(jnp.int32)
    places[...] = hits.astype(F32).astype(BF16)


def flow_kernel(wide, high, state, rate, near, far, inner, outer, out, grid, rates):
    feats = state.shape[1]
    span, across = high + 2 * STEPS, wide + 2 * STEPS
    half = span // 2
    odd, core = lax.rem(lax.axis_index("row"), 2), lax.axis_index("col")
    at = lax.broadcasted_iota(jnp.int32, (8, feats + 128), 0)
    low = jnp.where(core == 0, at, 7 - at) < STEPS
    for i in range(half):
        one = inner[i * 8 : i * 8 + 8].astype(F32)
        two = outer[i * 8 : i * 8 + 8].astype(F32)
        this = jnp.where(low, one, two)
        that = pltpu.roll(jnp.where(low, two, one), STEPS, 0)
        for r, tile in ((i, this), (i + half, that)):
            grid[0, r, wide:] = tile[:, :feats]
            rates[r, wide:] = tile[:, feats:]
    for r in range(high):
        grid[0, r, :wide] = state[r * wide : (r + 1) * wide]
        rates[r, :wide] = jnp.broadcast_to(rate[r * wide : (r + 1) * wide], (wide, 128))
    for at in range(STEPS):
        for ref, start in ((near, high + STEPS * odd), (far, high + STEPS * (1 - odd))):
            strip = ref[at * wide : (at + 1) * wide].astype(F32)
            grid[0, start + at, :wide] = strip[:, :feats]
            rates[start + at, :wide] = strip[:, feats:]
    for step in range(STEPS):
        now, later = step % 2, (step + 1) % 2
        margin = STEPS - 1 - step
        for r in [r % span for r in range(-margin, high + margin)]:
            here = grid[now, r]
            beside = (
                grid[now, (r - 1) % span]
                + grid[now, (r + 1) % span]
                + pltpu.roll(here, 1, 0)
                + pltpu.roll(here, across - 1, 0)
            )
            amount = rates[r]
            amount = jnp.concatenate([amount] * (feats // 128), axis=1)
            here = here + amount * (beside - 4.0 * here)
            if step == STEPS - 1:
                out[r * wide : (r + 1) * wide] = here[:wide]
            else:
                grid[later, r] = here


def physics_kernel(chunk, w_in, w_out, back, act_out, dpre_out):
    feats, hidden = w_in.shape
    cols = chunk[:, :feats]
    dtend = (0.5 * chunk[:, feats:].astype(F32)).astype(BF16)
    tend = adjoint = None
    piece = 256
    for h in range(0, hidden, piece):
        win, wout = w_in[:, h : h + piece], w_out[:, h : h + piece]
        pre = nn(cols, win)
        dact = nn(dtend, wout)
        sigma = 1.0 / (1.0 + jnp.exp(-pre))
        act = (pre * sigma).astype(BF16)
        dpre = (dact * (sigma * (1.0 + pre * (1.0 - sigma)))).astype(BF16)
        act_out[:, h : h + piece] = act
        dpre_out[:, h : h + piece] = dpre
        tend_h, adj_h = nt(act, wout), nt(dpre, win)
        tend = tend_h if tend is None else tend + tend_h
        adjoint = adj_h if adjoint is None else adjoint + adj_h
    back[:, :feats] = tend.astype(BF16)
    back[:, feats:] = adjoint.astype(BF16)


def first_physics_kernel(chunk, w_in_far, w_out_far, back, act_out, dpre_out, w_in, w_out, sems):
    copies = [
        pltpu.make_async_copy(w_in_far, w_in, sems.at[0]),
        pltpu.make_async_copy(w_out_far, w_out, sems.at[1]),
    ]
    for copy in copies:
        copy.start()
    for copy in copies:
        copy.wait()
    physics_kernel(chunk, w_in, w_out, back, act_out, dpre_out)


def grads_of(chunks, acts, dpres, h, piece, feats):
    dpre = jnp.concatenate([d[:, h : h + piece] for d in dpres], axis=0)
    act = jnp.concatenate([a[:, h : h + piece] for a in acts], axis=0)
    return dpre, act


def grads_kernel(owners, *refs):
    chunks, acts, dpres = refs[:owners], refs[owners : 2 * owners], refs[2 * owners : 3 * owners]
    keep, send = refs[3 * owners :]
    feats = chunks[0].shape[1] // 2
    hidden = acts[0].shape[1]
    block = keep.shape[2]
    cols = jnp.concatenate([c[:, :feats] for c in chunks], axis=0).T
    cots = jnp.concatenate([c[:, feats:] for c in chunks], axis=0)
    dtend = (0.5 * cots.astype(F32)).astype(BF16).T
    core = lax.axis_index("col")
    piece = 256
    for h in range(0, hidden, piece):
        dpre, act = grads_of(chunks, acts, dpres, h, piece, feats)
        for which, total in ((0, nn(cols, dpre)), (1, nn(dtend, act))):
            for x in range(2):
                one = total[2 * x * block : (2 * x + 1) * block]
                two = total[(2 * x + 1) * block : (2 * x + 2) * block]
                keep[which, x, :, h : h + piece] = jnp.where(core == 0, one, two)
                send[which, x, :, h : h + piece] = jnp.where(core == 0, two, one).astype(BF16)


def whole_grads_kernel(owners, *refs):
    chunks, acts, dpres = refs[:owners], refs[owners : 2 * owners], refs[2 * owners : 3 * owners]
    out = refs[3 * owners]
    feats = chunks[0].shape[1] // 2
    cols = jnp.concatenate([c[:, :feats] for c in chunks], axis=0).T
    cots = jnp.concatenate([c[:, feats:] for c in chunks], axis=0)
    dtend = (0.5 * cots.astype(F32)).astype(BF16).T
    piece = 256
    for h in range(0, acts[0].shape[1], piece):
        dpre, act = grads_of(chunks, acts, dpres, h, piece, feats)
        out[:feats, h : h + piece] = nn(cols, dpre)
        out[feats:, h : h + piece] = nn(dtend, act)


def share_kernel(keep, got, mine, *sends):
    row = lax.axis_index("row")
    y, x = lax.div(row, 2), lax.rem(row, 2)
    mine[...] = keep[y, x] + got[y, x].astype(F32)
    for send, (dy, dx) in zip(sends, ((0, 1), (1, 0), (1, 1))):
        send[...] = (keep[y ^ dy, x ^ dx] + got[y ^ dy, x ^ dx].astype(F32)).astype(BF16)


def gather_kernel(mine, one, two, three, out):
    rows, hidden = mine.shape
    for j in range(hidden // 128):
        at = slice(j * 128, (j + 1) * 128)
        total = mine[:, at] + one[:, at].astype(F32) + (two[:, at].astype(F32) + three[:, at].astype(F32))
        out[pl.ds(j, rows, stride=hidden // 128), :] = total


def finish_kernel(owners, field, places, *refs):
    backs, new_state, column_adjoint = refs[:owners], refs[owners], refs[owners + 1]
    feats = field.shape[1]
    cap = backs[0].shape[0]
    rows = nn(places[...], jnp.concatenate([b[...] for b in backs], axis=0))
    new_state[...] = field[...] + 0.5 * rows[:, :feats]
    column_adjoint[...] = rows[:, feats:].astype(BF16)


def swap(axis, bit):
    return [(i, i ^ bit) for i in range(lax.axis_size(axis))]


def partners(k):
    owners, cores = lax.axis_size("grp"), lax.axis_size("col")
    return [
        (g * cores + c, (g ^ (k if c == 0 else owners - k)) * cores + c)
        for g in range(owners)
        for c in range(cores)
    ]


def outward(axis):
    count = lax.axis_size(axis)
    return [(i, (i + 2 * (i % 2) - 1) % count) for i in range(count)]


def local(state, rate, cotangent, dest, w_in, w_out):
    high, wide, feats = state.shape
    count = high * wide
    owners = lax.axis_size("grp")
    cap = 2 * count // owners
    hidden = w_in.shape[2]
    flat_state = state.reshape(count, feats)
    flat_cot = cotangent.reshape(count, feats)

    strip = shape((STEPS * wide, feats + 128), BF16)
    *chunks, inner, outer, rate_col, place_row = call(
        functools.partial(pack_kernel, owners, cap, wide, high),
        [dest.reshape(1, count), rate, flat_state, flat_cot],
        [shape((cap, 2 * feats), BF16)] * owners + [strip, strip, shape((count, 1), F32), shape((1, count), jnp.int32)],
        [
            pltpu.VMEM((1, count), jnp.int32),
            pltpu.VMEM((high, wide), F32),
            pltpu.VMEM((count, feats), F32),
            pltpu.VMEM((count, feats), BF16),
            pltpu.SemaphoreType.DMA((4,)),
        ],
        far=(0, 1, 2, 3),
        vmem=60 << 20,
    )
    got = [chunks[0]] + [None] * (owners - 1)
    for k in range(owners - 1, 0, -1):
        got[k] = lax.ppermute(chunks[k], ("grp", "col"), partners(k))
    near = lax.ppermute(inner, "row", swap("row", 1))
    far = lax.ppermute(outer, "row", outward("row"))

    backs, acts, dpres = [None] * owners, [None] * owners, [None] * owners

    def physics(k, after=()):
        made = [shape((cap, 2 * feats), BF16)] + [shape((cap, hidden), BF16)] * 2
        backs[k], acts[k], dpres[k] = call(
            physics_kernel, [got[k], weight_in, weight_out], made, after=after
        )
        backs[k] = lax.ppermute(backs[k], ("grp", "col"), partners(k))
        return (acts[k],)

    weight = shape((feats, hidden), BF16)
    backs[0], acts[0], dpres[0], weight_in, weight_out = call(
        first_physics_kernel,
        [chunks[0], w_in[0], w_out[0]],
        [shape((cap, 2 * feats), BF16)] + [shape((cap, hidden), BF16)] * 2 + [weight, weight],
        [pltpu.SemaphoreType.DMA((2,))],
        far=(1, 2),
    )
    done = (acts[0],)
    side = shape(((high + 2 * STEPS) * STEPS, feats + 128), BF16)
    inner, outer, places = call(
        functools.partial(edge_kernel, wide, high),
        [flat_state, rate_col, near, far, place_row],
        [side, side, shape((count, owners * cap), BF16)],
        after=done,
    )
    inner_back = lax.ppermute(inner, "col", swap("col", 1))
    outer_back = lax.ppermute(outer, ("grp", "col"), outward(("grp", "col")))
    done = (places,)
    for k in (1, 2, 3, *range(4, owners)):
        done = physics(k, done)

    parts = lax.axis_size("row") * lax.axis_size("col")
    block = 2 * feats // parts
    if lax.axis_size("row") == 4 and lax.axis_size("col") == 2:
        keep, send = call(
            functools.partial(grads_kernel, owners),
            [*got, *acts, *dpres],
            [shape((2, 2, block, hidden), F32), shape((2, 2, block, hidden), BF16)],
        )
        arrived = lax.ppermute(send, "col", swap("col", 1))
        mine, *shares = call(
            share_kernel,
            [keep, arrived],
            [shape((block, hidden), F32)] + [shape((block, hidden), BF16)] * 3,
        )
        done = (mine,)
        shares = [lax.ppermute(s, "row", swap("row", bit + 1)) for bit, s in enumerate(shares)]
        (summed,) = call(
            gather_kernel, [mine, *shares], [shape((block * hidden // 128, 128), F32)]
        )
    else:
        (flat,) = call(
            functools.partial(whole_grads_kernel, owners),
            [*got, *acts, *dpres],
            [shape((2 * feats, hidden), F32)],
        )
        done = (flat,)
        summed = lax.psum_scatter(
            flat.reshape(-1, 128), ("row", "col"), scatter_dimension=0, tiled=True
        )
    (field,) = call(
        functools.partial(flow_kernel, wide, high),
        [flat_state, rate_col, near, far, inner_back, outer_back],
        [shape((count, feats), F32)],
        [
            pltpu.VMEM((2, high + 2 * STEPS, wide + 2 * STEPS, feats), F32),
            pltpu.VMEM((high + 2 * STEPS, wide + 2 * STEPS, 128), F32),
        ],
        after=done,
    )
    new_state, column_adjoint = call(
        functools.partial(finish_kernel, owners),
        [field, places, *backs],
        [shape((count, feats), F32), shape((count, feats), BF16)],
    )
    return (
        new_state.reshape(state.shape),
        column_adjoint.reshape(state.shape),
        summed[None],
    )


def solution(mesh):
    in_specs = (
        P("row", ("grp", "col"), None),
        P("row", ("grp", "col")),
        P("row", ("grp", "col"), None),
        P("row", ("grp", "col"), None, None),
        P("grp", None, None),
        P("grp", None, None),
    )
    out_specs = (
        P("row", ("grp", "col"), None),
        P("row", ("grp", "col"), None),
        P("grp", ("row", "col"), None),
    )
    return jax.shard_map(local, mesh=mesh, in_specs=in_specs, out_specs=out_specs, check_vma=False)
```

```python
import functools

import jax
import jax.numpy as jnp
from jax import lax
from jax.experimental import pallas as pl
from jax.experimental.pallas import tpu as pltpu
from jax.sharding import PartitionSpec as P

STEPS = 4
BF16 = jnp.bfloat16
F32 = jnp.float32
VMEM = pl.BlockSpec(memory_space=pltpu.VMEM)
HBM = pl.BlockSpec(memory_space=pltpu.HBM)
ANY = pl.BlockSpec(memory_space=pl.ANY)


def call(kernel, ins, outs, scratch=(), after=(), far=(), vmem=24 << 20, flops=None):
    ins = [pltpu.with_memory_space_constraint(x, pltpu.HBM) if n in far else x for n, x in enumerate(ins)]
    specs = [HBM if n in far else VMEM for n in range(len(ins))]
    count = len(ins)

    def body(*refs):
        kernel(*refs[:count], *refs[count + len(after) :])

    return pl.pallas_call(
        body,
        out_shape=list(outs),
        in_specs=specs + [ANY] * len(after),
        out_specs=[VMEM] * len(outs),
        scratch_shapes=list(scratch),
        compiler_params=pltpu.CompilerParams(vmem_limit_bytes=vmem),
        cost_estimate=flops and pl.CostEstimate(flops=flops, bytes_accessed=0, transcendentals=0),
    )(*ins, *after)


def shape(dims, dtype):
    return jax.ShapeDtypeStruct(dims, dtype)


def nt(a, b):
    return lax.dot_general(a, b, (((1,), (1,)), ((), ())), preferred_element_type=F32)


def nn(a, b):
    return jnp.dot(a, b, preferred_element_type=F32)


def pack_kernel(owners, cap, wide, high, *refs):
    far, near, sems = refs[:4], refs[-5:-1], refs[-1]
    chunks, inner, outer, rate_cols, places = refs[4 : owners + 4], *refs[owners + 4 : -5]
    copies = [pltpu.make_async_copy(a, b, sems.at[n]) for n, (a, b) in enumerate(zip(far, near))]
    for copy in copies:
        copy.start()
    dest, rate, state, cot = near
    count, feats = state.shape
    copies[0].wait()
    named = lax.broadcasted_iota(jnp.int32, (max(8, owners), count), 0) == dest[...]
    earlier = lax.broadcasted_iota(jnp.int32, (count, count), 0) < lax.broadcasted_iota(
        jnp.int32, (count, count), 1
    )
    ranks = nn(named.astype(F32).astype(BF16), earlier.astype(F32).astype(BF16))
    slot = jnp.sum(jnp.where(named, ranks, 0.0), axis=0, keepdims=True).astype(jnp.int32)
    ahead = dest[...] - lax.axis_index("grp")
    turn = jnp.where(lax.axis_index("col") == 0, -ahead, ahead)
    place = jnp.where(turn < 0, turn + owners, turn) * cap + slot
    places[...] = place
    for copy in copies[1:]:
        copy.wait()
    turned = rate[...].T
    for r in range(high):
        rate_cols[r * wide : (r + 1) * wide] = turned[:, r : r + 1]
    cols = state[...].astype(BF16)
    cots = cot[...]
    for k in range(owners):
        rows = lax.broadcasted_iota(jnp.int32, (cap, count), 0) + k * cap
        placing = (rows == place).astype(F32).astype(BF16)
        chunks[k][:, :feats] = nn(placing, cols).astype(BF16)
        chunks[k][:, feats:] = nn(placing, cots).astype(BF16)
    strip = STEPS * wide
    odd = lax.rem(lax.axis_index("row"), 2)
    for out, top in ((inner, odd), (outer, 1 - odd)):
        start = pl.multiple_of((1 - top) * (count - strip), strip)
        out[:, :feats] = state[pl.ds(start, strip)].astype(BF16)
        out[:, feats:] = jnp.broadcast_to(rate_cols[pl.ds(start, strip)], (strip, 128)).astype(BF16)


def edge_kernel(wide, high, state, rate, near, far, place_row, inner, outer, places):
    feats = state.shape[1]
    span = high + 2 * STEPS
    half = span // 2
    odd, core = lax.rem(lax.axis_index("row"), 2), lax.axis_index("col")
    low = lax.broadcasted_iota(jnp.int32, (8, feats + 128), 0) < STEPS
    tiles = []
    for r in range(span):
        if r < high:
            first = [
                jnp.concatenate(
                    [
                        state[r * wide + c : r * wide + c + 8],
                        jnp.broadcast_to(rate[r * wide + c : r * wide + c + 8], (8, 128)),
                    ],
                    axis=1,
                )
                for c in (0, wide - 8)
            ]
        else:
            at = slice((r - high) % STEPS * wide, ((r - high) % STEPS + 1) * wide)
            is_near = (odd == 0) if r < high + STEPS else (odd == 1)
            both = jnp.where(is_near, near[at].astype(F32), far[at].astype(F32))
            first = [both[:8], both[wide - 8 :]]
        tiles.append(jnp.where(low, first[0], first[1]))
    lefts, rights = [], []
    for i in range(half):
        turned = pltpu.roll(tiles[i + half], STEPS, 0)
        lefts.append(jnp.where(low, tiles[i], turned))
        rights.append(jnp.where(low, turned, tiles[i]))
    for i in range(0, half, 2):
        one = jnp.concatenate(lefts[i : i + 2], axis=0)
        two = jnp.concatenate(rights[i : i + 2], axis=0)
        inner[i * 8 : i * 8 + 16] = jnp.where(core == 0, two, one).astype(BF16)
        outer[i * 8 : i * 8 + 16] = jnp.where(core == 0, one, two).astype(BF16)
    count = state.shape[0]
    same = lax.broadcasted_iota(jnp.int32, (count, count), 0) == lax.broadcasted_iota(
        jnp.int32, (count, count), 1
    )
    place = jnp.sum(jnp.where(same, place_row[...], 0).astype(F32), axis=1, keepdims=True)
    hits = lax.broadcasted_iota(jnp.int32, places.shape, 1) == place.astype(jnp.int32)
    places[...] = hits.astype(F32).astype(BF16)


def flow_kernel(wide, high, state, rate, near, far, inner, outer, out, grid, rates):
    feats = state.shape[1]
    span, across = high + 2 * STEPS, wide + 2 * STEPS
    half = span // 2
    odd, core = lax.rem(lax.axis_index("row"), 2), lax.axis_index("col")
    at = lax.broadcasted_iota(jnp.int32, (8, feats + 128), 0)
    low = jnp.where(core == 0, at, 7 - at) < STEPS
    for i in range(half):
        one = inner[i * 8 : i * 8 + 8].astype(F32)
        two = outer[i * 8 : i * 8 + 8].astype(F32)
        this = jnp.where(low, one, two)
        that = pltpu.roll(jnp.where(low, two, one), STEPS, 0)
        for r, tile in ((i, this), (i + half, that)):
            grid[0, r, wide:] = tile[:, :feats]
            rates[r, wide:] = tile[:, feats:]
    for r in range(high):
        grid[0, r, :wide] = state[r * wide : (r + 1) * wide]
        rates[r, :wide] = jnp.broadcast_to(rate[r * wide : (r + 1) * wide], (wide, 128))
    for at in range(STEPS):
        for ref, start in ((near, high + STEPS * odd), (far, high + STEPS * (1 - odd))):
            strip = ref[at * wide : (at + 1) * wide].astype(F32)
            grid[0, start + at, :wide] = strip[:, :feats]
            rates[start + at, :wide] = strip[:, feats:]
    for step in range(STEPS):
        now, later = step % 2, (step + 1) % 2
        margin = STEPS - 1 - step
        for r in [r % span for r in range(-margin, high + margin)]:
            here = grid[now, r]
            beside = (
                grid[now, (r - 1) % span]
                + grid[now, (r + 1) % span]
                + pltpu.roll(here, 1, 0)
                + pltpu.roll(here, across - 1, 0)
            )
            amount = rates[r]
            amount = jnp.concatenate([amount] * (feats // 128), axis=1)
            here = here + amount * (beside - 4.0 * here)
            if step == STEPS - 1:
                out[r * wide : (r + 1) * wide] = here[:wide]
            else:
                grid[later, r] = here


def physics_kernel(chunk, w_in, w_out, back, act_out, dpre_out):
    feats, hidden = w_in.shape
    cols = chunk[:, :feats]
    dtend = (0.5 * chunk[:, feats:].astype(F32)).astype(BF16)
    tend = adjoint = None
    piece = 256
    for h in range(0, hidden, piece):
        win, wout = w_in[:, h : h + piece], w_out[:, h : h + piece]
        pre = nn(cols, win)
        dact = nn(dtend, wout)
        sigma = 1.0 / (1.0 + jnp.exp(-pre))
        act = (pre * sigma).astype(BF16)
        dpre = (dact * (sigma * (1.0 + pre * (1.0 - sigma)))).astype(BF16)
        act_out[:, h : h + piece] = act
        dpre_out[:, h : h + piece] = dpre
        tend_h, adj_h = nt(act, wout), nt(dpre, win)
        tend = tend_h if tend is None else tend + tend_h
        adjoint = adj_h if adjoint is None else adjoint + adj_h
    back[:, :feats] = tend.astype(BF16)
    back[:, feats:] = adjoint.astype(BF16)


def first_physics_kernel(chunk, w_in_far, w_out_far, back, act_out, dpre_out, w_in, w_out, sems):
    feats, hidden = w_in.shape
    piece = feats // 4
    copies = [
        pltpu.make_async_copy(far.at[at], near.at[at], sems.at[n, r])
        for r, at in enumerate(pl.ds(r * piece, piece) for r in range(4))
        for n, (far, near) in enumerate(((w_in_far, w_in), (w_out_far, w_out)))
    ]
    for copy in copies:
        copy.start()
    for copy in copies:
        copy.wait()
    physics_kernel(chunk, w_in, w_out, back, act_out, dpre_out)


def grads_of(chunks, acts, dpres, h, piece, feats):
    dpre = jnp.concatenate([d[:, h : h + piece] for d in dpres], axis=0)
    act = jnp.concatenate([a[:, h : h + piece] for a in acts], axis=0)
    return dpre, act


def grads_kernel(owners, *refs):
    chunks, acts, dpres = refs[:owners], refs[owners : 2 * owners], refs[2 * owners : 3 * owners]
    keep, send = refs[3 * owners :]
    feats = chunks[0].shape[1] // 2
    hidden = acts[0].shape[1]
    block = keep.shape[2]
    cols = jnp.concatenate([c[:, :feats] for c in chunks], axis=0).T
    cots = jnp.concatenate([c[:, feats:] for c in chunks], axis=0)
    dtend = (0.5 * cots.astype(F32)).astype(BF16).T
    core = lax.axis_index("col")
    piece = 256
    for h in range(0, hidden, piece):
        dpre, act = grads_of(chunks, acts, dpres, h, piece, feats)
        for which, total in ((0, nn(cols, dpre)), (1, nn(dtend, act))):
            for x in range(2):
                one = total[2 * x * block : (2 * x + 1) * block]
                two = total[(2 * x + 1) * block : (2 * x + 2) * block]
                keep[which, x, :, h : h + piece] = jnp.where(core == 0, one, two)
                send[which, x, :, h : h + piece] = jnp.where(core == 0, two, one).astype(BF16)


def whole_grads_kernel(owners, *refs):
    chunks, acts, dpres = refs[:owners], refs[owners : 2 * owners], refs[2 * owners : 3 * owners]
    out = refs[3 * owners]
    feats = chunks[0].shape[1] // 2
    cols = jnp.concatenate([c[:, :feats] for c in chunks], axis=0).T
    cots = jnp.concatenate([c[:, feats:] for c in chunks], axis=0)
    dtend = (0.5 * cots.astype(F32)).astype(BF16).T
    piece = 256
    for h in range(0, acts[0].shape[1], piece):
        dpre, act = grads_of(chunks, acts, dpres, h, piece, feats)
        out[:feats, h : h + piece] = nn(cols, dpre)
        out[feats:, h : h + piece] = nn(dtend, act)


def gap_kernel(out):
    out[...] = jnp.zeros_like(out)


def share_kernel(keep, got, mine, *sends):
    row = lax.axis_index("row")
    y, x = lax.div(row, 2), lax.rem(row, 2)
    mine[...] = keep[y, x] + got[y, x].astype(F32)
    for send, (dy, dx) in zip(sends, ((0, 1), (1, 0), (1, 1))):
        send[...] = (keep[y ^ dy, x ^ dx] + got[y ^ dy, x ^ dx].astype(F32)).astype(BF16)


def gather_kernel(mine, one, two, three, out):
    rows, hidden = mine.shape
    for j in range(hidden // 128):
        at = slice(j * 128, (j + 1) * 128)
        total = mine[:, at] + one[:, at].astype(F32) + (two[:, at].astype(F32) + three[:, at].astype(F32))
        out[pl.ds(j, rows, stride=hidden // 128), :] = total


def finish_kernel(owners, field, places, *refs):
    backs, new_state, column_adjoint = refs[:owners], refs[owners], refs[owners + 1]
    feats = field.shape[1]
    cap = backs[0].shape[0]
    rows = nn(places[...], jnp.concatenate([b[...] for b in backs], axis=0))
    new_state[...] = field[...] + 0.5 * rows[:, :feats]
    column_adjoint[...] = rows[:, feats:].astype(BF16)


def swap(axis, bit):
    return [(i, i ^ bit) for i in range(lax.axis_size(axis))]


def partners(k):
    owners, cores = lax.axis_size("grp"), lax.axis_size("col")
    pairs = [(g * cores, (g - k) % owners * cores + 1) for g in range(owners)]
    return pairs + [(b, a) for a, b in pairs]


def outward(axis):
    count = lax.axis_size(axis)
    return [(i, (i + 2 * (i % 2) - 1) % count) for i in range(count)]


def local(state, rate, cotangent, dest, w_in, w_out):
    high, wide, feats = state.shape
    count = high * wide
    owners = lax.axis_size("grp")
    cap = 2 * count // owners
    hidden = w_in.shape[2]
    flat_state = state.reshape(count, feats)
    flat_cot = cotangent.reshape(count, feats)

    strip = shape((STEPS * wide, feats + 128), BF16)
    *chunks, inner, outer, rate_col, place_row = call(
        functools.partial(pack_kernel, owners, cap, wide, high),
        [dest.reshape(1, count), rate, flat_state, flat_cot],
        [shape((cap, 2 * feats), BF16)] * owners + [strip, strip, shape((count, 1), F32), shape((1, count), jnp.int32)],
        [
            pltpu.VMEM((1, count), jnp.int32),
            pltpu.VMEM((high, wide), F32),
            pltpu.VMEM((count, feats), F32),
            pltpu.VMEM((count, feats), BF16),
            pltpu.SemaphoreType.DMA((4,)),
        ],
        far=(0, 1, 2, 3),
    )
    got = [chunks[0]] + [None] * (owners - 1)
    for k in range(owners - 1, 0, -1):
        got[k] = lax.ppermute(chunks[k], ("grp", "col"), partners(k))
    near = lax.ppermute(inner, "row", swap("row", 1))
    far = lax.ppermute(outer, "row", outward("row"))

    backs, acts, dpres = [None] * owners, [None] * owners, [None] * owners

    def physics(k, after=()):
        made = [shape((cap, 2 * feats), BF16)] + [shape((cap, hidden), BF16)] * 2
        backs[k], acts[k], dpres[k] = call(
            physics_kernel, [got[k], weight_in, weight_out], made, after=after
        )
        backs[k] = lax.ppermute(backs[k], ("grp", "col"), partners(k))
        return (acts[k],)

    weight = shape((feats, hidden), BF16)
    backs[0], acts[0], dpres[0], weight_in, weight_out = call(
        first_physics_kernel,
        [chunks[0], w_in[0], w_out[0]],
        [shape((cap, 2 * feats), BF16)] + [shape((cap, hidden), BF16)] * 2 + [weight, weight],
        [pltpu.SemaphoreType.DMA((2, 4))],
        far=(1, 2),
    )
    done = (acts[0],)
    side = shape(((high + 2 * STEPS) * STEPS, feats + 128), BF16)
    inner, outer, places = call(
        functools.partial(edge_kernel, wide, high),
        [flat_state, rate_col, near, far, place_row],
        [side, side, shape((count, owners * cap), BF16)],
        after=done,
    )
    outer_back = lax.ppermute(outer, ("grp", "col"), outward(("grp", "col")))
    inner_back = lax.ppermute(inner, "col", swap("col", 1))
    done = (places,)
    for k in (1, 2, 3, *range(4, owners)):
        done = physics(k, done)

    parts = lax.axis_size("row") * lax.axis_size("col")
    block = 2 * feats // parts
    if lax.axis_size("row") == 4 and lax.axis_size("col") == 2:
        keep, send = call(
            functools.partial(grads_kernel, owners),
            [*got, *acts, *dpres],
            [shape((2, 2, block, hidden), F32), shape((2, 2, block, hidden), BF16)],
        )
        arrived = lax.ppermute(send, "col", swap("col", 1))
        (gap,) = call(gap_kernel, [], [shape((8, 128), F32)], after=(keep,), flops=10000000000)
        mine, *shares = call(
            share_kernel,
            [keep, arrived],
            [shape((block, hidden), F32)] + [shape((block, hidden), BF16)] * 3,
            after=(gap,),
        )
        done = (mine,)
        shares = [lax.ppermute(s, "row", swap("row", bit + 1)) for bit, s in enumerate(shares)]
        (summed,) = call(
            gather_kernel, [mine, *shares], [shape((block * hidden // 128, 128), F32)]
        )
    else:
        (flat,) = call(
            functools.partial(whole_grads_kernel, owners),
            [*got, *acts, *dpres],
            [shape((2 * feats, hidden), F32)],
        )
        done = (flat,)
        summed = lax.psum_scatter(
            flat.reshape(-1, 128), ("row", "col"), scatter_dimension=0, tiled=True
        )
    (field,) = call(
        functools.partial(flow_kernel, wide, high),
        [flat_state, rate_col, near, far, inner_back, outer_back],
        [shape((count, feats), F32)],
        [
            pltpu.VMEM((2, high + 2 * STEPS, wide + 2 * STEPS, feats), F32),
            pltpu.VMEM((high + 2 * STEPS, wide + 2 * STEPS, 128), F32),
        ],
        after=done,
    )
    new_state, column_adjoint = call(
        functools.partial(finish_kernel, owners),
        [field, places, *backs],
        [shape((count, feats), F32), shape((count, feats), BF16)],
    )
    return (
        new_state.reshape(state.shape),
        column_adjoint.reshape(state.shape),
        summed[None],
    )


def solution(mesh):
    in_specs = (
        P("row", ("grp", "col"), None),
        P("row", ("grp", "col")),
        P("row", ("grp", "col"), None),
        P("row", ("grp", "col"), None, None),
        P("grp", None, None),
        P("grp", None, None),
    )
    out_specs = (
        P("row", ("grp", "col"), None),
        P("row", ("grp", "col"), None),
        P("grp", ("row", "col"), None),
    )
    return jax.shard_map(local, mesh=mesh, in_specs=in_specs, out_specs=out_specs, check_vma=False)
```

```python
import functools

import jax
import jax.numpy as jnp
from jax import lax
from jax.experimental import pallas as pl
from jax.experimental.pallas import tpu as pltpu
from jax.sharding import PartitionSpec as P

STEPS = 4
BF16 = jnp.bfloat16
F32 = jnp.float32
VMEM = pl.BlockSpec(memory_space=pltpu.VMEM)
HBM = pl.BlockSpec(memory_space=pltpu.HBM)
ANY = pl.BlockSpec(memory_space=pl.ANY)


def call(kernel, ins, outs, scratch=(), after=(), far=(), vmem=24 << 20, flops=None):
    ins = [pltpu.with_memory_space_constraint(x, pltpu.HBM) if n in far else x for n, x in enumerate(ins)]
    specs = [HBM if n in far else VMEM for n in range(len(ins))]
    count = len(ins)

    def body(*refs):
        kernel(*refs[:count], *refs[count + len(after) :])

    return pl.pallas_call(
        body,
        out_shape=list(outs),
        in_specs=specs + [ANY] * len(after),
        out_specs=[VMEM] * len(outs),
        scratch_shapes=list(scratch),
        compiler_params=pltpu.CompilerParams(vmem_limit_bytes=vmem),
        cost_estimate=flops and pl.CostEstimate(flops=flops, bytes_accessed=0, transcendentals=0),
    )(*ins, *after)


def shape(dims, dtype):
    return jax.ShapeDtypeStruct(dims, dtype)


def nt(a, b):
    return lax.dot_general(a, b, (((1,), (1,)), ((), ())), preferred_element_type=F32)


def nn(a, b):
    return jnp.dot(a, b, preferred_element_type=F32)


def pack_kernel(owners, cap, wide, high, *refs):
    far, near, sems = refs[:6], [*refs[-5:-1], *refs[-7:-5]], refs[-1]
    chunks, inner, outer, rate_cols, places = refs[6 : owners + 6], *refs[owners + 6 : -7]
    copies = [pltpu.make_async_copy(a, b, sems.at[n]) for n, (a, b) in enumerate(zip(far, near))]
    for copy in copies:
        copy.start()
    dest, rate, state, cot, _, _ = near
    count, feats = state.shape
    copies[0].wait()
    named = lax.broadcasted_iota(jnp.int32, (max(8, owners), count), 0) == dest[...]
    earlier = lax.broadcasted_iota(jnp.int32, (count, count), 0) < lax.broadcasted_iota(
        jnp.int32, (count, count), 1
    )
    ranks = nn(named.astype(F32).astype(BF16), earlier.astype(F32).astype(BF16))
    slot = jnp.sum(jnp.where(named, ranks, 0.0), axis=0, keepdims=True).astype(jnp.int32)
    ahead = dest[...] - lax.axis_index("grp")
    turn = jnp.where(lax.axis_index("col") == 0, -ahead, ahead)
    place = jnp.where(turn < 0, turn + owners, turn) * cap + slot
    places[...] = place
    for copy in copies[1:4]:
        copy.wait()
    turned = rate[...].T
    for r in range(high):
        rate_cols[r * wide : (r + 1) * wide] = turned[:, r : r + 1]
    cols = state[...].astype(BF16)
    cots = cot[...]
    for k in range(owners):
        rows = lax.broadcasted_iota(jnp.int32, (cap, count), 0) + k * cap
        placing = (rows == place).astype(F32).astype(BF16)
        chunks[k][:, :feats] = nn(placing, cols).astype(BF16)
        chunks[k][:, feats:] = nn(placing, cots).astype(BF16)
    strip = STEPS * wide
    odd = lax.rem(lax.axis_index("row"), 2)
    for out, top in ((inner, odd), (outer, 1 - odd)):
        start = pl.multiple_of((1 - top) * (count - strip), strip)
        out[:, :feats] = state[pl.ds(start, strip)].astype(BF16)
        out[:, feats:] = jnp.broadcast_to(rate_cols[pl.ds(start, strip)], (strip, 128)).astype(BF16)
    for copy in copies[4:]:
        copy.wait()


def edge_kernel(wide, high, state, rate, near, far, place_row, inner, outer, places):
    feats = state.shape[1]
    span = high + 2 * STEPS
    half = span // 2
    odd, core = lax.rem(lax.axis_index("row"), 2), lax.axis_index("col")
    low = lax.broadcasted_iota(jnp.int32, (8, feats + 128), 0) < STEPS
    tiles = []
    for r in range(span):
        if r < high:
            first = [
                jnp.concatenate(
                    [
                        state[r * wide + c : r * wide + c + 8],
                        jnp.broadcast_to(rate[r * wide + c : r * wide + c + 8], (8, 128)),
                    ],
                    axis=1,
                )
                for c in (0, wide - 8)
            ]
        else:
            at = slice((r - high) % STEPS * wide, ((r - high) % STEPS + 1) * wide)
            is_near = (odd == 0) if r < high + STEPS else (odd == 1)
            both = jnp.where(is_near, near[at].astype(F32), far[at].astype(F32))
            first = [both[:8], both[wide - 8 :]]
        tiles.append(jnp.where(low, first[0], first[1]))
    lefts, rights = [], []
    for i in range(half):
        turned = pltpu.roll(tiles[i + half], STEPS, 0)
        lefts.append(jnp.where(low, tiles[i], turned))
        rights.append(jnp.where(low, turned, tiles[i]))
    for i in range(0, half, 2):
        one = jnp.concatenate(lefts[i : i + 2], axis=0)
        two = jnp.concatenate(rights[i : i + 2], axis=0)
        inner[i * 8 : i * 8 + 16] = jnp.where(core == 0, two, one).astype(BF16)
        outer[i * 8 : i * 8 + 16] = jnp.where(core == 0, one, two).astype(BF16)
    count = state.shape[0]
    same = lax.broadcasted_iota(jnp.int32, (count, count), 0) == lax.broadcasted_iota(
        jnp.int32, (count, count), 1
    )
    place = jnp.sum(jnp.where(same, place_row[...], 0).astype(F32), axis=1, keepdims=True)
    hits = lax.broadcasted_iota(jnp.int32, places.shape, 1) == place.astype(jnp.int32)
    places[...] = hits.astype(F32).astype(BF16)


def flow_kernel(wide, high, state, rate, near, far, inner, outer, out, grid, rates):
    feats = state.shape[1]
    span, across = high + 2 * STEPS, wide + 2 * STEPS
    half = span // 2
    odd, core = lax.rem(lax.axis_index("row"), 2), lax.axis_index("col")
    at = lax.broadcasted_iota(jnp.int32, (8, feats + 128), 0)
    low = jnp.where(core == 0, at, 7 - at) < STEPS
    for i in range(half):
        one = inner[i * 8 : i * 8 + 8].astype(F32)
        two = outer[i * 8 : i * 8 + 8].astype(F32)
        this = jnp.where(low, one, two)
        that = pltpu.roll(jnp.where(low, two, one), STEPS, 0)
        for r, tile in ((i, this), (i + half, that)):
            grid[0, r, wide:] = tile[:, :feats]
            rates[r, wide:] = tile[:, feats:]
    for r in range(high):
        grid[0, r, :wide] = state[r * wide : (r + 1) * wide]
        rates[r, :wide] = jnp.broadcast_to(rate[r * wide : (r + 1) * wide], (wide, 128))
    for at in range(STEPS):
        for ref, start in ((near, high + STEPS * odd), (far, high + STEPS * (1 - odd))):
            strip = ref[at * wide : (at + 1) * wide].astype(F32)
            grid[0, start + at, :wide] = strip[:, :feats]
            rates[start + at, :wide] = strip[:, feats:]
    for step in range(STEPS):
        now, later = step % 2, (step + 1) % 2
        margin = STEPS - 1 - step
        for r in [r % span for r in range(-margin, high + margin)]:
            here = grid[now, r]
            beside = (
                grid[now, (r - 1) % span]
                + grid[now, (r + 1) % span]
                + pltpu.roll(here, 1, 0)
                + pltpu.roll(here, across - 1, 0)
            )
            amount = rates[r]
            amount = jnp.concatenate([amount] * (feats // 128), axis=1)
            here = here + amount * (beside - 4.0 * here)
            if step == STEPS - 1:
                out[r * wide : (r + 1) * wide] = here[:wide]
            else:
                grid[later, r] = here


def physics_kernel(chunk, w_in, w_out, back, act_out, dpre_out):
    feats, hidden = w_in.shape
    cols = chunk[:, :feats]
    dtend = (0.5 * chunk[:, feats:].astype(F32)).astype(BF16)
    tend = adjoint = None
    piece = hidden
    for h in range(0, hidden, piece):
        win, wout = w_in[:, h : h + piece], w_out[:, h : h + piece]
        pre = nn(cols, win)
        dact = nn(dtend, wout)
        sigma = 1.0 / (1.0 + jnp.exp(-pre))
        act = (pre * sigma).astype(BF16)
        dpre = (dact * (sigma * (1.0 + pre * (1.0 - sigma)))).astype(BF16)
        act_out[:, h : h + piece] = act
        dpre_out[:, h : h + piece] = dpre
        tend_h, adj_h = nt(act, wout), nt(dpre, win)
        tend = tend_h if tend is None else tend + tend_h
        adjoint = adj_h if adjoint is None else adjoint + adj_h
    back[:, :feats] = tend.astype(BF16)
    back[:, feats:] = adjoint.astype(BF16)


def grads_of(chunks, acts, dpres, h, piece, feats):
    dpre = jnp.concatenate([d[:, h : h + piece] for d in dpres], axis=0)
    act = jnp.concatenate([a[:, h : h + piece] for a in acts], axis=0)
    return dpre, act


def grads_kernel(owners, *refs):
    chunks, acts, dpres = refs[:owners], refs[owners : 2 * owners], refs[2 * owners : 3 * owners]
    keep, send = refs[3 * owners :]
    feats = chunks[0].shape[1] // 2
    hidden = acts[0].shape[1]
    block = keep.shape[2]
    cols = jnp.concatenate([c[:, :feats] for c in chunks], axis=0).T
    cots = jnp.concatenate([c[:, feats:] for c in chunks], axis=0)
    dtend = (0.5 * cots.astype(F32)).astype(BF16).T
    core = lax.axis_index("col")
    piece = 512
    for h in range(0, hidden, piece):
        dpre, act = grads_of(chunks, acts, dpres, h, piece, feats)
        for which, total in ((0, nn(cols, dpre)), (1, nn(dtend, act))):
            for x in range(2):
                one = total[2 * x * block : (2 * x + 1) * block]
                two = total[(2 * x + 1) * block : (2 * x + 2) * block]
                keep[which, x, :, h : h + piece] = jnp.where(core == 0, one, two)
                send[which, x, :, h : h + piece] = jnp.where(core == 0, two, one).astype(BF16)


def whole_grads_kernel(owners, *refs):
    chunks, acts, dpres = refs[:owners], refs[owners : 2 * owners], refs[2 * owners : 3 * owners]
    out = refs[3 * owners]
    feats = chunks[0].shape[1] // 2
    cols = jnp.concatenate([c[:, :feats] for c in chunks], axis=0).T
    cots = jnp.concatenate([c[:, feats:] for c in chunks], axis=0)
    dtend = (0.5 * cots.astype(F32)).astype(BF16).T
    piece = 256
    for h in range(0, acts[0].shape[1], piece):
        dpre, act = grads_of(chunks, acts, dpres, h, piece, feats)
        out[:feats, h : h + piece] = nn(cols, dpre)
        out[feats:, h : h + piece] = nn(dtend, act)


def gap_kernel(out):
    out[...] = jnp.zeros_like(out)


def share_kernel(keep, got, mine, *sends):
    row = lax.axis_index("row")
    y, x = lax.div(row, 2), lax.rem(row, 2)
    mine[...] = keep[y, x] + got[y, x].astype(F32)
    for send, (dy, dx) in zip(sends, ((0, 1), (1, 0), (1, 1))):
        send[...] = (keep[y ^ dy, x ^ dx] + got[y ^ dy, x ^ dx].astype(F32)).astype(BF16)


def gather_kernel(mine, one, two, three, out):
    rows, hidden = mine.shape
    for j in range(hidden // 128):
        at = slice(j * 128, (j + 1) * 128)
        total = mine[:, at] + one[:, at].astype(F32) + (two[:, at].astype(F32) + three[:, at].astype(F32))
        out[pl.ds(j, rows, stride=hidden // 128), :] = total


def finish_kernel(owners, field, places, *refs):
    backs, new_state, column_adjoint = refs[:owners], refs[owners], refs[owners + 1]
    feats = field.shape[1]
    cap = backs[0].shape[0]
    rows = nn(places[...], jnp.concatenate([b[...] for b in backs], axis=0))
    new_state[...] = field[...] + 0.5 * rows[:, :feats]
    column_adjoint[...] = rows[:, feats:].astype(BF16)


def swap(axis, bit):
    return [(i, i ^ bit) for i in range(lax.axis_size(axis))]


def partners(k):
    owners, cores = lax.axis_size("grp"), lax.axis_size("col")
    pairs = [(g * cores, (g - k) % owners * cores + 1) for g in range(owners)]
    return pairs + [(b, a) for a, b in pairs]


def outward(axis):
    count = lax.axis_size(axis)
    return [(i, (i + 2 * (i % 2) - 1) % count) for i in range(count)]


def local(state, rate, cotangent, dest, w_in, w_out):
    high, wide, feats = state.shape
    count = high * wide
    owners = lax.axis_size("grp")
    cap = 2 * count // owners
    hidden = w_in.shape[2]
    flat_state = state.reshape(count, feats)
    flat_cot = cotangent.reshape(count, feats)

    weight = shape((feats, hidden), BF16)
    strip = shape((STEPS * wide, feats + 128), BF16)
    *chunks, inner, outer, rate_col, place_row, weight_in, weight_out = call(
        functools.partial(pack_kernel, owners, cap, wide, high),
        [dest.reshape(1, count), rate, flat_state, flat_cot, w_in[0], w_out[0]],
        [shape((cap, 2 * feats), BF16)] * owners + [strip, strip, shape((count, 1), F32), shape((1, count), jnp.int32), weight, weight],
        [
            pltpu.VMEM((1, count), jnp.int32),
            pltpu.VMEM((high, wide), F32),
            pltpu.VMEM((count, feats), F32),
            pltpu.VMEM((count, feats), BF16),
            pltpu.SemaphoreType.DMA((6,)),
        ],
        far=(0, 1, 2, 3, 4, 5),
    )
    got = [chunks[0]] + [None] * (owners - 1)
    for k in range(owners - 1, 0, -1):
        got[k] = lax.ppermute(chunks[k], ("grp", "col"), partners(k))
    near = lax.ppermute(inner, "row", swap("row", 1))
    far = lax.ppermute(outer, "row", outward("row"))

    backs, acts, dpres = [None] * owners, [None] * owners, [None] * owners

    def physics(k, after=()):
        made = [shape((cap, 2 * feats), BF16)] + [shape((cap, hidden), BF16)] * 2
        backs[k], acts[k], dpres[k] = call(
            physics_kernel, [got[k], weight_in, weight_out], made, after=after
        )
        if k > 0:
            backs[k] = lax.ppermute(backs[k], ("grp", "col"), partners(k))
        return (acts[k],)

    physics(0)
    done = (acts[0],)
    side = shape(((high + 2 * STEPS) * STEPS, feats + 128), BF16)
    inner, outer, places = call(
        functools.partial(edge_kernel, wide, high),
        [flat_state, rate_col, near, far, place_row],
        [side, side, shape((count, owners * cap), BF16)],
        after=done,
    )
    outer_back = lax.ppermute(outer, ("grp", "col"), outward(("grp", "col")))
    inner_back = lax.ppermute(inner, "col", swap("col", 1))
    done = (places,)
    for k in (3, 2, 1, *range(4, owners)):
        done = physics(k, done)

    parts = lax.axis_size("row") * lax.axis_size("col")
    block = 2 * feats // parts
    if lax.axis_size("row") == 4 and lax.axis_size("col") == 2:
        keep, send = call(
            functools.partial(grads_kernel, owners),
            [*got, *acts, *dpres],
            [shape((2, 2, block, hidden), F32), shape((2, 2, block, hidden), BF16)],
        )
        arrived = lax.ppermute(send, "col", swap("col", 1))
        (gap,) = call(gap_kernel, [], [shape((8, 128), F32)], after=(keep,), flops=10000000000)
        mine, *shares = call(
            share_kernel,
            [keep, arrived],
            [shape((block, hidden), F32)] + [shape((block, hidden), BF16)] * 3,
            after=(gap,),
        )
        done = (mine,)
        shares = [lax.ppermute(s, "row", swap("row", bit + 1)) for bit, s in enumerate(shares)]
        (summed,) = call(
            gather_kernel, [mine, *shares], [shape((block * hidden // 128, 128), F32)]
        )
    else:
        (flat,) = call(
            functools.partial(whole_grads_kernel, owners),
            [*got, *acts, *dpres],
            [shape((2 * feats, hidden), F32)],
        )
        done = (flat,)
        summed = lax.psum_scatter(
            flat.reshape(-1, 128), ("row", "col"), scatter_dimension=0, tiled=True
        )
    (field,) = call(
        functools.partial(flow_kernel, wide, high),
        [flat_state, rate_col, near, far, inner_back, outer_back],
        [shape((count, feats), F32)],
        [
            pltpu.VMEM((2, high + 2 * STEPS, wide + 2 * STEPS, feats), F32),
            pltpu.VMEM((high + 2 * STEPS, wide + 2 * STEPS, 128), F32),
        ],
        after=done,
    )
    new_state, column_adjoint = call(
        functools.partial(finish_kernel, owners),
        [field, places, *backs],
        [shape((count, feats), F32), shape((count, feats), BF16)],
    )
    return (
        new_state.reshape(state.shape),
        column_adjoint.reshape(state.shape),
        summed[None],
    )


def solution(mesh):
    in_specs = (
        P("row", ("grp", "col"), None),
        P("row", ("grp", "col")),
        P("row", ("grp", "col"), None),
        P("row", ("grp", "col"), None, None),
        P("grp", None, None),
        P("grp", None, None),
    )
    out_specs = (
        P("row", ("grp", "col"), None),
        P("row", ("grp", "col"), None),
        P("grp", ("row", "col"), None),
    )
    return jax.shard_map(local, mesh=mesh, in_specs=in_specs, out_specs=out_specs, check_vma=False)
```

```python
import functools

import jax
import jax.numpy as jnp
from jax import lax
from jax.experimental import pallas as pl
from jax.experimental.pallas import tpu as pltpu
from jax.sharding import PartitionSpec as P

STEPS = 4
BF16 = jnp.bfloat16
F32 = jnp.float32
VMEM = pl.BlockSpec(memory_space=pltpu.VMEM)
HBM = pl.BlockSpec(memory_space=pltpu.HBM)
ANY = pl.BlockSpec(memory_space=pl.ANY)


def call(kernel, ins, outs, scratch=(), after=(), far=(), vmem=24 << 20, flops=None):
    ins = [pltpu.with_memory_space_constraint(x, pltpu.HBM) if n in far else x for n, x in enumerate(ins)]
    specs = [HBM if n in far else VMEM for n in range(len(ins))]
    count = len(ins)

    def body(*refs):
        kernel(*refs[:count], *refs[count + len(after) :])

    return pl.pallas_call(
        body,
        out_shape=list(outs),
        in_specs=specs + [ANY] * len(after),
        out_specs=[VMEM] * len(outs),
        scratch_shapes=list(scratch),
        compiler_params=pltpu.CompilerParams(vmem_limit_bytes=vmem),
        cost_estimate=flops and pl.CostEstimate(flops=flops, bytes_accessed=0, transcendentals=0),
    )(*ins, *after)


def shape(dims, dtype):
    return jax.ShapeDtypeStruct(dims, dtype)


def nt(a, b):
    return lax.dot_general(a, b, (((1,), (1,)), ((), ())), preferred_element_type=F32)


def nn(a, b):
    return jnp.dot(a, b, preferred_element_type=F32)


def pack_kernel(owners, cap, wide, high, *refs):
    far, near, sems = refs[:6], [*refs[-5:-1], *refs[-7:-5]], refs[-1]
    chunks, inner, outer, rate_cols, places = refs[6 : owners + 6], *refs[owners + 6 : -7]
    copies = [pltpu.make_async_copy(a, b, sems.at[n]) for n, (a, b) in enumerate(zip(far, near))]
    for copy in copies:
        copy.start()
    dest, rate, state, cot, _, _ = near
    count, feats = state.shape
    copies[0].wait()
    named = lax.broadcasted_iota(jnp.int32, (max(8, owners), count), 0) == dest[...]
    earlier = lax.broadcasted_iota(jnp.int32, (count, count), 0) < lax.broadcasted_iota(
        jnp.int32, (count, count), 1
    )
    ranks = nn(named.astype(F32).astype(BF16), earlier.astype(F32).astype(BF16))
    slot = jnp.sum(jnp.where(named, ranks, 0.0), axis=0, keepdims=True).astype(jnp.int32)
    ahead = dest[...] - lax.axis_index("grp")
    turn = jnp.where(lax.axis_index("col") == 0, -ahead, ahead)
    place = jnp.where(turn < 0, turn + owners, turn) * cap + slot
    places[...] = place
    for copy in copies[1:4]:
        copy.wait()
    turned = rate[...].T
    for r in range(high):
        rate_cols[r * wide : (r + 1) * wide] = turned[:, r : r + 1]
    cols = state[...].astype(BF16)
    cots = cot[...]
    for k in range(owners):
        rows = lax.broadcasted_iota(jnp.int32, (cap, count), 0) + k * cap
        placing = (rows == place).astype(F32).astype(BF16)
        chunks[k][:, :feats] = nn(placing, cols).astype(BF16)
        chunks[k][:, feats:] = nn(placing, cots).astype(BF16)
    strip = STEPS * wide
    odd = lax.rem(lax.axis_index("row"), 2)
    for out, top in ((inner, odd), (outer, 1 - odd)):
        start = pl.multiple_of((1 - top) * (count - strip), strip)
        out[:, :feats] = state[pl.ds(start, strip)].astype(BF16)
        out[:, feats:] = jnp.broadcast_to(rate_cols[pl.ds(start, strip)], (strip, 128)).astype(BF16)
    for copy in copies[4:]:
        copy.wait()


def edge_kernel(wide, high, state, rate, near, far, place_row, inner, outer, places):
    feats = state.shape[1]
    span = high + 2 * STEPS
    half = span // 2
    odd, core = lax.rem(lax.axis_index("row"), 2), lax.axis_index("col")
    low = lax.broadcasted_iota(jnp.int32, (8, feats + 128), 0) < STEPS
    tiles = []
    for r in range(span):
        if r < high:
            first = [
                jnp.concatenate(
                    [
                        state[r * wide + c : r * wide + c + 8],
                        jnp.broadcast_to(rate[r * wide + c : r * wide + c + 8], (8, 128)),
                    ],
                    axis=1,
                )
                for c in (0, wide - 8)
            ]
        else:
            at = slice((r - high) % STEPS * wide, ((r - high) % STEPS + 1) * wide)
            is_near = (odd == 0) if r < high + STEPS else (odd == 1)
            both = jnp.where(is_near, near[at].astype(F32), far[at].astype(F32))
            first = [both[:8], both[wide - 8 :]]
        tiles.append(jnp.where(low, first[0], first[1]))
    lefts, rights = [], []
    for i in range(half):
        turned = pltpu.roll(tiles[i + half], STEPS, 0)
        lefts.append(jnp.where(low, tiles[i], turned))
        rights.append(jnp.where(low, turned, tiles[i]))
    for i in range(0, half, 2):
        one = jnp.concatenate(lefts[i : i + 2], axis=0)
        two = jnp.concatenate(rights[i : i + 2], axis=0)
        inner[i * 8 : i * 8 + 16] = jnp.where(core == 0, two, one).astype(BF16)
        outer[i * 8 : i * 8 + 16] = jnp.where(core == 0, one, two).astype(BF16)
    count = state.shape[0]
    same = lax.broadcasted_iota(jnp.int32, (count, count), 0) == lax.broadcasted_iota(
        jnp.int32, (count, count), 1
    )
    place = jnp.sum(jnp.where(same, place_row[...], 0).astype(F32), axis=1, keepdims=True)
    hits = lax.broadcasted_iota(jnp.int32, places.shape, 1) == place.astype(jnp.int32)
    places[...] = hits.astype(F32).astype(BF16)


def flow_kernel(wide, high, state, rate, near, far, inner, outer, out, grid, rates):
    feats = state.shape[1]
    span, across = high + 2 * STEPS, wide + 2 * STEPS
    half = span // 2
    odd, core = lax.rem(lax.axis_index("row"), 2), lax.axis_index("col")
    at = lax.broadcasted_iota(jnp.int32, (8, feats + 128), 0)
    low = jnp.where(core == 0, at, 7 - at) < STEPS
    for i in range(half):
        one = inner[i * 8 : i * 8 + 8].astype(F32)
        two = outer[i * 8 : i * 8 + 8].astype(F32)
        this = jnp.where(low, one, two)
        that = pltpu.roll(jnp.where(low, two, one), STEPS, 0)
        for r, tile in ((i, this), (i + half, that)):
            grid[0, r, wide:] = tile[:, :feats]
            rates[r, wide:] = tile[:, feats:]
    for r in range(high):
        grid[0, r, :wide] = state[r * wide : (r + 1) * wide]
        rates[r, :wide] = jnp.broadcast_to(rate[r * wide : (r + 1) * wide], (wide, 128))
    for at in range(STEPS):
        for ref, start in ((near, high + STEPS * odd), (far, high + STEPS * (1 - odd))):
            strip = ref[at * wide : (at + 1) * wide].astype(F32)
            grid[0, start + at, :wide] = strip[:, :feats]
            rates[start + at, :wide] = strip[:, feats:]
    for step in range(STEPS):
        now, later = step % 2, (step + 1) % 2
        margin = STEPS - 1 - step
        for r in [r % span for r in range(-margin, high + margin)]:
            here = grid[now, r]
            beside = (
                grid[now, (r - 1) % span]
                + grid[now, (r + 1) % span]
                + pltpu.roll(here, 1, 0)
                + pltpu.roll(here, across - 1, 0)
            )
            amount = rates[r]
            amount = jnp.concatenate([amount] * (feats // 128), axis=1)
            here = here + amount * (beside - 4.0 * here)
            if step == STEPS - 1:
                out[r * wide : (r + 1) * wide] = here[:wide]
            else:
                grid[later, r] = here


def physics_kernel(chunk, w_in, w_out, back, act_out, dpre_out):
    feats, hidden = w_in.shape
    cols = chunk[:, :feats]
    dtend = (0.5 * chunk[:, feats:].astype(F32)).astype(BF16)
    tend = adjoint = None
    piece = hidden
    for h in range(0, hidden, piece):
        win, wout = w_in[:, h : h + piece], w_out[:, h : h + piece]
        pre = nn(cols, win)
        dact = nn(dtend, wout)
        sigma = 1.0 / (1.0 + jnp.exp(-pre))
        act = (pre * sigma).astype(BF16)
        dpre = (dact * (sigma * (1.0 + pre * (1.0 - sigma)))).astype(BF16)
        act_out[:, h : h + piece] = act
        dpre_out[:, h : h + piece] = dpre
        tend_h, adj_h = nt(act, wout), nt(dpre, win)
        tend = tend_h if tend is None else tend + tend_h
        adjoint = adj_h if adjoint is None else adjoint + adj_h
    back[:, :feats] = tend.astype(BF16)
    back[:, feats:] = adjoint.astype(BF16)


def grads_of(chunks, acts, dpres, h, piece, feats):
    dpre = jnp.concatenate([d[:, h : h + piece] for d in dpres], axis=0)
    act = jnp.concatenate([a[:, h : h + piece] for a in acts], axis=0)
    return dpre, act


def grads_kernel(owners, *refs):
    chunks, acts, dpres = refs[:owners], refs[owners : 2 * owners], refs[2 * owners : 3 * owners]
    keep, send = refs[3 * owners :]
    feats = chunks[0].shape[1] // 2
    hidden = acts[0].shape[1]
    block = keep.shape[2]
    cols = jnp.concatenate([c[:, :feats] for c in chunks], axis=0).T
    cots = jnp.concatenate([c[:, feats:] for c in chunks], axis=0)
    dtend = (0.5 * cots.astype(F32)).astype(BF16).T
    core = lax.axis_index("col")
    piece = 512
    for h in range(0, hidden, piece):
        dpre, act = grads_of(chunks, acts, dpres, h, piece, feats)
        for which, total in ((0, nn(cols, dpre)), (1, nn(dtend, act))):
            for x in range(2):
                one = total[2 * x * block : (2 * x + 1) * block]
                two = total[(2 * x + 1) * block : (2 * x + 2) * block]
                keep[which, x, :, h : h + piece] = jnp.where(core == 0, one, two)
                send[which, x, :, h : h + piece] = jnp.where(core == 0, two, one).astype(BF16)


def whole_grads_kernel(owners, *refs):
    chunks, acts, dpres = refs[:owners], refs[owners : 2 * owners], refs[2 * owners : 3 * owners]
    out = refs[3 * owners]
    feats = chunks[0].shape[1] // 2
    cols = jnp.concatenate([c[:, :feats] for c in chunks], axis=0).T
    cots = jnp.concatenate([c[:, feats:] for c in chunks], axis=0)
    dtend = (0.5 * cots.astype(F32)).astype(BF16).T
    piece = 256
    for h in range(0, acts[0].shape[1], piece):
        dpre, act = grads_of(chunks, acts, dpres, h, piece, feats)
        out[:feats, h : h + piece] = nn(cols, dpre)
        out[feats:, h : h + piece] = nn(dtend, act)


def gap_kernel(out):
    out[...] = jnp.zeros_like(out)


def share_kernel(keep, got, mine, *sends):
    row = lax.axis_index("row")
    y, x = lax.div(row, 2), lax.rem(row, 2)
    mine[...] = keep[y, x] + got[y, x].astype(F32)
    for send, (dy, dx) in zip(sends, ((1, 1), (0, 1), (1, 0))):
        send[...] = (keep[y ^ dy, x ^ dx] + got[y ^ dy, x ^ dx].astype(F32)).astype(BF16)


def gather_kernel(mine, one, two, three, out):
    rows, hidden = mine.shape
    for j in range(hidden // 128):
        at = slice(j * 128, (j + 1) * 128)
        total = mine[:, at] + one[:, at].astype(F32) + (two[:, at].astype(F32) + three[:, at].astype(F32))
        out[pl.ds(j, rows, stride=hidden // 128), :] = total


def finish_kernel(owners, field, places, *refs):
    backs, new_state, column_adjoint = refs[:owners], refs[owners], refs[owners + 1]
    feats = field.shape[1]
    cap = backs[0].shape[0]
    rows = nn(places[...], jnp.concatenate([b[...] for b in backs], axis=0))
    new_state[...] = field[...] + 0.5 * rows[:, :feats]
    column_adjoint[...] = rows[:, feats:].astype(BF16)


def swap(axis, bit):
    return [(i, i ^ bit) for i in range(lax.axis_size(axis))]


def partners(k):
    owners, cores = lax.axis_size("grp"), lax.axis_size("col")
    pairs = [(g * cores, (g - k) % owners * cores + 1) for g in range(owners)]
    return pairs + [(b, a) for a, b in pairs]


def outward(axis):
    count = lax.axis_size(axis)
    return [(i, (i + 2 * (i % 2) - 1) % count) for i in range(count)]


def local(state, rate, cotangent, dest, w_in, w_out):
    high, wide, feats = state.shape
    count = high * wide
    owners = lax.axis_size("grp")
    cap = 2 * count // owners
    hidden = w_in.shape[2]
    flat_state = state.reshape(count, feats)
    flat_cot = cotangent.reshape(count, feats)

    weight = shape((feats, hidden), BF16)
    strip = shape((STEPS * wide, feats + 128), BF16)
    *chunks, inner, outer, rate_col, place_row, weight_in, weight_out = call(
        functools.partial(pack_kernel, owners, cap, wide, high),
        [dest.reshape(1, count), rate, flat_state, flat_cot, w_in[0], w_out[0]],
        [shape((cap, 2 * feats), BF16)] * owners + [strip, strip, shape((count, 1), F32), shape((1, count), jnp.int32), weight, weight],
        [
            pltpu.VMEM((1, count), jnp.int32),
            pltpu.VMEM((high, wide), F32),
            pltpu.VMEM((count, feats), F32),
            pltpu.VMEM((count, feats), BF16),
            pltpu.SemaphoreType.DMA((6,)),
        ],
        far=(0, 1, 2, 3, 4, 5),
    )
    got = [chunks[0]] + [None] * (owners - 1)
    for k in range(owners - 1, 0, -1):
        got[k] = lax.ppermute(chunks[k], ("grp", "col"), partners(k))
    far = lax.ppermute(outer, "row", outward("row"))
    near = lax.ppermute(inner, "row", swap("row", 1))

    backs, acts, dpres = [None] * owners, [None] * owners, [None] * owners

    def physics(k, after=()):
        made = [shape((cap, 2 * feats), BF16)] + [shape((cap, hidden), BF16)] * 2
        backs[k], acts[k], dpres[k] = call(
            physics_kernel, [got[k], weight_in, weight_out], made, after=after
        )
        if k > 0:
            backs[k] = lax.ppermute(backs[k], ("grp", "col"), partners(k))
        return (acts[k],)

    physics(0)
    done = (acts[0],)
    side = shape(((high + 2 * STEPS) * STEPS, feats + 128), BF16)
    inner, outer, places = call(
        functools.partial(edge_kernel, wide, high),
        [flat_state, rate_col, near, far, place_row],
        [side, side, shape((count, owners * cap), BF16)],
        after=done,
    )
    outer_back = lax.ppermute(outer, ("grp", "col"), outward(("grp", "col")))
    inner_back = lax.ppermute(inner, "col", swap("col", 1))
    done = (places,)
    for k in (3, 2, 1, *range(4, owners)):
        done = physics(k, done)

    parts = lax.axis_size("row") * lax.axis_size("col")
    block = 2 * feats // parts
    if lax.axis_size("row") == 4 and lax.axis_size("col") == 2:
        keep, send = call(
            functools.partial(grads_kernel, owners),
            [*got, *acts, *dpres],
            [shape((2, 2, block, hidden), F32), shape((2, 2, block, hidden), BF16)],
        )
        arrived = lax.ppermute(send, "col", swap("col", 1))
        (gap,) = call(gap_kernel, [], [shape((8, 128), F32)], after=(keep,), flops=10000000000)
        mine, *shares = call(
            share_kernel,
            [keep, arrived],
            [shape((block, hidden), F32)] + [shape((block, hidden), BF16)] * 3,
            after=(gap,),
        )
        done = (mine,)
        shares = [lax.ppermute(s, "row", swap("row", bit)) for bit, s in zip((3, 1, 2), shares)]
        (summed,) = call(
            gather_kernel, [mine, *shares], [shape((block * hidden // 128, 128), F32)]
        )
    else:
        (flat,) = call(
            functools.partial(whole_grads_kernel, owners),
            [*got, *acts, *dpres],
            [shape((2 * feats, hidden), F32)],
        )
        done = (flat,)
        summed = lax.psum_scatter(
            flat.reshape(-1, 128), ("row", "col"), scatter_dimension=0, tiled=True
        )
    (field,) = call(
        functools.partial(flow_kernel, wide, high),
        [flat_state, rate_col, near, far, inner_back, outer_back],
        [shape((count, feats), F32)],
        [
            pltpu.VMEM((2, high + 2 * STEPS, wide + 2 * STEPS, feats), F32),
            pltpu.VMEM((high + 2 * STEPS, wide + 2 * STEPS, 128), F32),
        ],
        after=done,
    )
    new_state, column_adjoint = call(
        functools.partial(finish_kernel, owners),
        [field, places, *backs],
        [shape((count, feats), F32), shape((count, feats), BF16)],
    )
    return (
        new_state.reshape(state.shape),
        column_adjoint.reshape(state.shape),
        summed[None],
    )


def solution(mesh):
    in_specs = (
        P("row", ("grp", "col"), None),
        P("row", ("grp", "col")),
        P("row", ("grp", "col"), None),
        P("row", ("grp", "col"), None, None),
        P("grp", None, None),
        P("grp", None, None),
    )
    out_specs = (
        P("row", ("grp", "col"), None),
        P("row", ("grp", "col"), None),
        P("grp", ("row", "col"), None),
    )
    return jax.shard_map(local, mesh=mesh, in_specs=in_specs, out_specs=out_specs, check_vma=False)
```

```python
import functools

import jax
import jax.numpy as jnp
from jax import lax
from jax.experimental import pallas as pl
from jax.experimental.pallas import tpu as pltpu
from jax.sharding import PartitionSpec as P

STEPS = 4
BF16 = jnp.bfloat16
F32 = jnp.float32
VMEM = pl.BlockSpec(memory_space=pltpu.VMEM)
HBM = pl.BlockSpec(memory_space=pltpu.HBM)
ANY = pl.BlockSpec(memory_space=pl.ANY)


def call(kernel, ins, outs, scratch=(), after=(), far=(), vmem=24 << 20, flops=None):
    ins = [pltpu.with_memory_space_constraint(x, pltpu.HBM) if n in far else x for n, x in enumerate(ins)]
    specs = [HBM if n in far else VMEM for n in range(len(ins))]
    count = len(ins)

    def body(*refs):
        kernel(*refs[:count], *refs[count + len(after) :])

    return pl.pallas_call(
        body,
        out_shape=list(outs),
        in_specs=specs + [ANY] * len(after),
        out_specs=[VMEM] * len(outs),
        scratch_shapes=list(scratch),
        compiler_params=pltpu.CompilerParams(vmem_limit_bytes=vmem),
        cost_estimate=flops and pl.CostEstimate(flops=flops, bytes_accessed=0, transcendentals=0),
    )(*ins, *after)


def shape(dims, dtype):
    return jax.ShapeDtypeStruct(dims, dtype)


def nt(a, b):
    return lax.dot_general(a, b, (((1,), (1,)), ((), ())), preferred_element_type=F32)


def nn(a, b):
    return jnp.dot(a, b, preferred_element_type=F32)


def pack_kernel(owners, cap, wide, high, *refs):
    far, near, sems = refs[:6], [*refs[-5:-1], *refs[-7:-5]], refs[-1]
    chunks, inner, outer, rate_cols, places = refs[6 : owners + 6], *refs[owners + 6 : -7]
    copies = [pltpu.make_async_copy(a, b, sems.at[n]) for n, (a, b) in enumerate(zip(far, near))]
    for copy in copies:
        copy.start()
    dest, rate, state, cot, _, _ = near
    count, feats = state.shape
    copies[0].wait()
    named = lax.broadcasted_iota(jnp.int32, (max(8, owners), count), 0) == dest[...]
    earlier = lax.broadcasted_iota(jnp.int32, (count, count), 0) < lax.broadcasted_iota(
        jnp.int32, (count, count), 1
    )
    ranks = nn(named.astype(F32).astype(BF16), earlier.astype(F32).astype(BF16))
    slot = jnp.sum(jnp.where(named, ranks, 0.0), axis=0, keepdims=True).astype(jnp.int32)
    ahead = dest[...] - lax.axis_index("grp")
    turn = jnp.where(lax.axis_index("col") == 0, -ahead, ahead)
    place = jnp.where(turn < 0, turn + owners, turn) * cap + slot
    places[...] = place
    for copy in copies[1:4]:
        copy.wait()
    turned = rate[...].T
    for r in range(high):
        rate_cols[r * wide : (r + 1) * wide] = turned[:, r : r + 1]
    cols = state[...].astype(BF16)
    cots = cot[...]
    for k in range(owners):
        rows = lax.broadcasted_iota(jnp.int32, (cap, count), 0) + k * cap
        placing = (rows == place).astype(F32).astype(BF16)
        chunks[k][:, :feats] = nn(placing, cols).astype(BF16)
        chunks[k][:, feats:] = nn(placing, cots).astype(BF16)
    strip = STEPS * wide
    odd = lax.rem(lax.axis_index("row"), 2)
    for out, top in ((inner, odd), (outer, 1 - odd)):
        start = pl.multiple_of((1 - top) * (count - strip), strip)
        out[:, :feats] = state[pl.ds(start, strip)].astype(BF16)
        out[:, feats:] = jnp.broadcast_to(rate_cols[pl.ds(start, strip)], (strip, 128)).astype(BF16)
    for copy in copies[4:]:
        copy.wait()


def edge_kernel(wide, high, state, rate, near, far, place_row, inner, outer, places):
    feats = state.shape[1]
    span = high + 2 * STEPS
    half = span // 2
    odd, core = lax.rem(lax.axis_index("row"), 2), lax.axis_index("col")
    low = lax.broadcasted_iota(jnp.int32, (8, feats + 128), 0) < STEPS
    tiles = []
    for r in range(span):
        if r < high:
            first = [
                jnp.concatenate(
                    [
                        state[r * wide + c : r * wide + c + 8],
                        jnp.broadcast_to(rate[r * wide + c : r * wide + c + 8], (8, 128)),
                    ],
                    axis=1,
                )
                for c in (0, wide - 8)
            ]
        else:
            at = slice((r - high) % STEPS * wide, ((r - high) % STEPS + 1) * wide)
            is_near = (odd == 0) if r < high + STEPS else (odd == 1)
            both = jnp.where(is_near, near[at].astype(F32), far[at].astype(F32))
            first = [both[:8], both[wide - 8 :]]
        tiles.append(jnp.where(low, first[0], first[1]))
    lefts, rights = [], []
    for i in range(half):
        turned = pltpu.roll(tiles[i + half], STEPS, 0)
        lefts.append(jnp.where(low, tiles[i], turned))
        rights.append(jnp.where(low, turned, tiles[i]))
    for i in range(0, half, 2):
        one = jnp.concatenate(lefts[i : i + 2], axis=0)
        two = jnp.concatenate(rights[i : i + 2], axis=0)
        inner[i * 8 : i * 8 + 16] = jnp.where(core == 0, two, one).astype(BF16)
        outer[i * 8 : i * 8 + 16] = jnp.where(core == 0, one, two).astype(BF16)
    count = state.shape[0]
    same = lax.broadcasted_iota(jnp.int32, (count, count), 0) == lax.broadcasted_iota(
        jnp.int32, (count, count), 1
    )
    place = jnp.sum(jnp.where(same, place_row[...], 0).astype(F32), axis=1, keepdims=True)
    hits = lax.broadcasted_iota(jnp.int32, places.shape, 1) == place.astype(jnp.int32)
    places[...] = hits.astype(F32).astype(BF16)


def flow_kernel(wide, high, state, rate, near, far, inner, outer, out, grid, rates):
    feats = state.shape[1]
    span, across = high + 2 * STEPS, wide + 2 * STEPS
    half = span // 2
    odd, core = lax.rem(lax.axis_index("row"), 2), lax.axis_index("col")
    at = lax.broadcasted_iota(jnp.int32, (8, feats + 128), 0)
    low = jnp.where(core == 0, at, 7 - at) < STEPS
    for i in range(half):
        one = inner[i * 8 : i * 8 + 8].astype(F32)
        two = outer[i * 8 : i * 8 + 8].astype(F32)
        this = jnp.where(low, one, two)
        that = pltpu.roll(jnp.where(low, two, one), STEPS, 0)
        for r, tile in ((i, this), (i + half, that)):
            grid[0, r, wide:] = tile[:, :feats]
            rates[r, wide:] = tile[:, feats:]
    for r in range(high):
        grid[0, r, :wide] = state[r * wide : (r + 1) * wide]
        rates[r, :wide] = jnp.broadcast_to(rate[r * wide : (r + 1) * wide], (wide, 128))
    for at in range(STEPS):
        for ref, start in ((near, high + STEPS * odd), (far, high + STEPS * (1 - odd))):
            strip = ref[at * wide : (at + 1) * wide].astype(F32)
            grid[0, start + at, :wide] = strip[:, :feats]
            rates[start + at, :wide] = strip[:, feats:]
    for step in range(STEPS):
        now, later = step % 2, (step + 1) % 2
        margin = STEPS - 1 - step
        for r in [r % span for r in range(-margin, high + margin)]:
            here = grid[now, r]
            beside = (
                grid[now, (r - 1) % span]
                + grid[now, (r + 1) % span]
                + pltpu.roll(here, 1, 0)
                + pltpu.roll(here, across - 1, 0)
            )
            amount = rates[r]
            amount = jnp.concatenate([amount] * (feats // 128), axis=1)
            here = here + amount * (beside - 4.0 * here)
            if step == STEPS - 1:
                out[r * wide : (r + 1) * wide] = here[:wide]
            else:
                grid[later, r] = here


def physics_kernel(chunk, w_in, w_out, back, act_out, dpre_out):
    feats, hidden = w_in.shape
    cols = chunk[:, :feats]
    dtend = (0.5 * chunk[:, feats:].astype(F32)).astype(BF16)
    tend = adjoint = None
    piece = hidden
    for h in range(0, hidden, piece):
        win, wout = w_in[:, h : h + piece], w_out[:, h : h + piece]
        pre = nn(cols, win)
        dact = nn(dtend, wout)
        sigma = 1.0 / (1.0 + jnp.exp(-pre))
        act = (pre * sigma).astype(BF16)
        dpre = (dact * (sigma * (1.0 + pre * (1.0 - sigma)))).astype(BF16)
        act_out[:, h : h + piece] = act
        dpre_out[:, h : h + piece] = dpre
        tend_h, adj_h = nt(act, wout), nt(dpre, win)
        tend = tend_h if tend is None else tend + tend_h
        adjoint = adj_h if adjoint is None else adjoint + adj_h
    back[:, :feats] = tend.astype(BF16)
    back[:, feats:] = adjoint.astype(BF16)


def hold_kernel(back, out):
    out[...] = back[...]


def grads_of(chunks, acts, dpres, h, piece, feats):
    dpre = jnp.concatenate([d[:, h : h + piece] for d in dpres], axis=0)
    act = jnp.concatenate([a[:, h : h + piece] for a in acts], axis=0)
    return dpre, act


def grads_kernel(owners, *refs):
    chunks, acts, dpres = refs[:owners], refs[owners : 2 * owners], refs[2 * owners : 3 * owners]
    keep, send = refs[3 * owners :]
    feats = chunks[0].shape[1] // 2
    hidden = acts[0].shape[1]
    block = keep.shape[2]
    cols = jnp.concatenate([c[:, :feats] for c in chunks], axis=0).T
    cots = jnp.concatenate([c[:, feats:] for c in chunks], axis=0)
    dtend = (0.5 * cots.astype(F32)).astype(BF16).T
    core = lax.axis_index("col")
    piece = 512
    for h in range(0, hidden, piece):
        dpre, act = grads_of(chunks, acts, dpres, h, piece, feats)
        for which, total in ((0, nn(cols, dpre)), (1, nn(dtend, act))):
            for x in range(2):
                one = total[2 * x * block : (2 * x + 1) * block]
                two = total[(2 * x + 1) * block : (2 * x + 2) * block]
                keep[which, x, :, h : h + piece] = jnp.where(core == 0, one, two)
                send[which, x, :, h : h + piece] = jnp.where(core == 0, two, one).astype(BF16)


def whole_grads_kernel(owners, *refs):
    chunks, acts, dpres = refs[:owners], refs[owners : 2 * owners], refs[2 * owners : 3 * owners]
    out = refs[3 * owners]
    feats = chunks[0].shape[1] // 2
    cols = jnp.concatenate([c[:, :feats] for c in chunks], axis=0).T
    cots = jnp.concatenate([c[:, feats:] for c in chunks], axis=0)
    dtend = (0.5 * cots.astype(F32)).astype(BF16).T
    piece = 256
    for h in range(0, acts[0].shape[1], piece):
        dpre, act = grads_of(chunks, acts, dpres, h, piece, feats)
        out[:feats, h : h + piece] = nn(cols, dpre)
        out[feats:, h : h + piece] = nn(dtend, act)


def gap_kernel(out):
    out[...] = jnp.zeros_like(out)


def share_kernel(keep, got, mine, *sends):
    row = lax.axis_index("row")
    y, x = lax.div(row, 2), lax.rem(row, 2)
    mine[...] = keep[y, x] + got[y, x].astype(F32)
    for send, (dy, dx) in zip(sends, ((1, 1), (0, 1), (1, 0))):
        send[...] = (keep[y ^ dy, x ^ dx] + got[y ^ dy, x ^ dx].astype(F32)).astype(BF16)


def gather_kernel(mine, one, two, three, out):
    rows, hidden = mine.shape
    for j in range(hidden // 128):
        at = slice(j * 128, (j + 1) * 128)
        total = mine[:, at] + one[:, at].astype(F32) + (two[:, at].astype(F32) + three[:, at].astype(F32))
        out[pl.ds(j, rows, stride=hidden // 128), :] = total


def finish_kernel(owners, field, places, *refs):
    backs, new_state, column_adjoint = refs[:owners], refs[owners], refs[owners + 1]
    feats = field.shape[1]
    cap = backs[0].shape[0]
    rows = nn(places[...], jnp.concatenate([b[...] for b in backs], axis=0))
    new_state[...] = field[...] + 0.5 * rows[:, :feats]
    column_adjoint[...] = rows[:, feats:].astype(BF16)


def swap(axis, bit):
    return [(i, i ^ bit) for i in range(lax.axis_size(axis))]


def partners(k):
    owners, cores = lax.axis_size("grp"), lax.axis_size("col")
    pairs = [(g * cores, (g - k) % owners * cores + 1) for g in range(owners)]
    return pairs + [(b, a) for a, b in pairs]


def outward(axis):
    count = lax.axis_size(axis)
    return [(i, (i + 2 * (i % 2) - 1) % count) for i in range(count)]


def local(state, rate, cotangent, dest, w_in, w_out):
    high, wide, feats = state.shape
    count = high * wide
    owners = lax.axis_size("grp")
    cap = 2 * count // owners
    hidden = w_in.shape[2]
    flat_state = state.reshape(count, feats)
    flat_cot = cotangent.reshape(count, feats)

    weight = shape((feats, hidden), BF16)
    strip = shape((STEPS * wide, feats + 128), BF16)
    *chunks, inner, outer, rate_col, place_row, weight_in, weight_out = call(
        functools.partial(pack_kernel, owners, cap, wide, high),
        [dest.reshape(1, count), rate, flat_state, flat_cot, w_in[0], w_out[0]],
        [shape((cap, 2 * feats), BF16)] * owners + [strip, strip, shape((count, 1), F32), shape((1, count), jnp.int32), weight, weight],
        [
            pltpu.VMEM((1, count), jnp.int32),
            pltpu.VMEM((high, wide), F32),
            pltpu.VMEM((count, feats), F32),
            pltpu.VMEM((count, feats), BF16),
            pltpu.SemaphoreType.DMA((6,)),
        ],
        far=(0, 1, 2, 3, 4, 5),
    )
    got = [chunks[0]] + [None] * (owners - 1)
    for k in range(owners - 1, 0, -1):
        got[k] = lax.ppermute(chunks[k], ("grp", "col"), partners(k))
    far = lax.ppermute(outer, "row", outward("row"))
    near = lax.ppermute(inner, "row", swap("row", 1))

    backs, acts, dpres = [None] * owners, [None] * owners, [None] * owners

    def physics(k, after=(), held=False):
        made = [shape((cap, 2 * feats), BF16)] + [shape((cap, hidden), BF16)] * 2
        backs[k], acts[k], dpres[k] = call(
            physics_kernel, [got[k], weight_in, weight_out], made, after=after
        )
        if k > 0 and not held:
            backs[k] = lax.ppermute(backs[k], ("grp", "col"), partners(k))
        return (acts[k],)

    physics(0)
    done = (acts[0],)
    done = physics(3, done, True)
    side = shape(((high + 2 * STEPS) * STEPS, feats + 128), BF16)
    inner, outer, places = call(
        functools.partial(edge_kernel, wide, high),
        [flat_state, rate_col, near, far, place_row],
        [side, side, shape((count, owners * cap), BF16)],
        after=done,
    )
    outer_back = lax.ppermute(outer, ("grp", "col"), outward(("grp", "col")))
    inner_back = lax.ppermute(inner, "col", swap("col", 1))
    done = (places,)
    (back,) = call(hold_kernel, [backs[3]], [shape(backs[3].shape, BF16)], after=(places,))
    backs[3] = lax.ppermute(back, ("grp", "col"), partners(3))
    done = physics(2, done)
    done = physics(1, done)
    for k in range(4, owners):
        done = physics(k, done)

    parts = lax.axis_size("row") * lax.axis_size("col")
    block = 2 * feats // parts
    if lax.axis_size("row") == 4 and lax.axis_size("col") == 2:
        keep, send = call(
            functools.partial(grads_kernel, owners),
            [*got, *acts, *dpres],
            [shape((2, 2, block, hidden), F32), shape((2, 2, block, hidden), BF16)],
        )
        arrived = lax.ppermute(send, "col", swap("col", 1))
        (gap,) = call(gap_kernel, [], [shape((8, 128), F32)], after=(keep,), flops=10000000000)
        mine, *shares = call(
            share_kernel,
            [keep, arrived],
            [shape((block, hidden), F32)] + [shape((block, hidden), BF16)] * 3,
            after=(gap,),
        )
        done = (mine,)
        shares = [lax.ppermute(s, "row", swap("row", bit)) for bit, s in zip((3, 1, 2), shares)]
        (summed,) = call(
            gather_kernel, [mine, *shares], [shape((block * hidden // 128, 128), F32)]
        )
    else:
        (flat,) = call(
            functools.partial(whole_grads_kernel, owners),
            [*got, *acts, *dpres],
            [shape((2 * feats, hidden), F32)],
        )
        done = (flat,)
        summed = lax.psum_scatter(
            flat.reshape(-1, 128), ("row", "col"), scatter_dimension=0, tiled=True
        )
    (field,) = call(
        functools.partial(flow_kernel, wide, high),
        [flat_state, rate_col, near, far, inner_back, outer_back],
        [shape((count, feats), F32)],
        [
            pltpu.VMEM((2, high + 2 * STEPS, wide + 2 * STEPS, feats), F32),
            pltpu.VMEM((high + 2 * STEPS, wide + 2 * STEPS, 128), F32),
        ],
        after=done,
    )
    new_state, column_adjoint = call(
        functools.partial(finish_kernel, owners),
        [field, places, *backs],
        [shape((count, feats), F32), shape((count, feats), BF16)],
    )
    return (
        new_state.reshape(state.shape),
        column_adjoint.reshape(state.shape),
        summed[None],
    )


def solution(mesh):
    in_specs = (
        P("row", ("grp", "col"), None),
        P("row", ("grp", "col")),
        P("row", ("grp", "col"), None),
        P("row", ("grp", "col"), None, None),
        P("grp", None, None),
        P("grp", None, None),
    )
    out_specs = (
        P("row", ("grp", "col"), None),
        P("row", ("grp", "col"), None),
        P("grp", ("row", "col"), None),
    )
    return jax.shard_map(local, mesh=mesh, in_specs=in_specs, out_specs=out_specs, check_vma=False)
```

```python
import functools

import jax
import jax.numpy as jnp
from jax import lax
from jax.experimental import pallas as pl
from jax.experimental.pallas import tpu as pltpu
from jax.sharding import PartitionSpec as P

STEPS = 4
BF16 = jnp.bfloat16
F32 = jnp.float32
VMEM = pl.BlockSpec(memory_space=pltpu.VMEM)
HBM = pl.BlockSpec(memory_space=pltpu.HBM)
ANY = pl.BlockSpec(memory_space=pl.ANY)


def call(kernel, ins, outs, scratch=(), after=(), far=(), vmem=24 << 20, flops=None):
    ins = [
        pltpu.with_memory_space_constraint(x, pltpu.HBM) if n in far else x
        for n, x in enumerate(ins)
    ]
    specs = [HBM if n in far else VMEM for n in range(len(ins))]
    count = len(ins)

    def body(*refs):
        kernel(*refs[:count], *refs[count + len(after) :])

    return pl.pallas_call(
        body,
        out_shape=list(outs),
        in_specs=specs + [ANY] * len(after),
        out_specs=[VMEM] * len(outs),
        scratch_shapes=list(scratch),
        compiler_params=pltpu.CompilerParams(vmem_limit_bytes=vmem),
        cost_estimate=flops and pl.CostEstimate(flops=flops, bytes_accessed=0, transcendentals=0),
    )(*ins, *after)


def shape(dims, dtype):
    return jax.ShapeDtypeStruct(dims, dtype)


def nt(a, b):
    return lax.dot_general(a, b, (((1,), (1,)), ((), ())), preferred_element_type=F32)


def nn(a, b):
    return jnp.dot(a, b, preferred_element_type=F32)


def pack_kernel(owners, cap, wide, high, *refs):
    far, near, sems = refs[:6], [*refs[-5:-1], *refs[-7:-5]], refs[-1]
    chunks, inner, outer, rate_cols, places = refs[6 : owners + 6], *refs[owners + 6 : -7]
    copies = [pltpu.make_async_copy(a, b, sems.at[n]) for n, (a, b) in enumerate(zip(far, near))]
    for copy in copies:
        copy.start()
    dest, rate, state, cot, _, _ = near
    count, feats = state.shape
    copies[0].wait()
    named = lax.broadcasted_iota(jnp.int32, (max(8, owners), count), 0) == dest[...]
    earlier = lax.broadcasted_iota(jnp.int32, (count, count), 0) < lax.broadcasted_iota(
        jnp.int32, (count, count), 1
    )
    ranks = nn(named.astype(F32).astype(BF16), earlier.astype(F32).astype(BF16))
    slot = jnp.sum(jnp.where(named, ranks, 0.0), axis=0, keepdims=True).astype(jnp.int32)
    ahead = dest[...] - lax.axis_index("grp")
    turn = jnp.where(lax.axis_index("col") == 0, -ahead, ahead)
    place = jnp.where(turn < 0, turn + owners, turn) * cap + slot
    places[...] = place
    for copy in copies[1:4]:
        copy.wait()
    turned = rate[...].T
    for r in range(high):
        rate_cols[r * wide : (r + 1) * wide] = turned[:, r : r + 1]
    cols = state[...].astype(BF16)
    cots = cot[...]
    for k in range(owners):
        rows = lax.broadcasted_iota(jnp.int32, (cap, count), 0) + k * cap
        placing = (rows == place).astype(F32).astype(BF16)
        chunks[k][:, :feats] = nn(placing, cols).astype(BF16)
        chunks[k][:, feats:] = nn(placing, cots).astype(BF16)
    strip = STEPS * wide
    odd = lax.rem(lax.axis_index("row"), 2)
    for out, top in ((inner, odd), (outer, 1 - odd)):
        start = pl.multiple_of((1 - top) * (count - strip), strip)
        out[:, :feats] = state[pl.ds(start, strip)].astype(BF16)
        out[:, feats:] = jnp.broadcast_to(rate_cols[pl.ds(start, strip)], (strip, 128)).astype(BF16)
    for copy in copies[4:]:
        copy.wait()


def edge_kernel(wide, high, state, rate, near, far, place_row, inner, outer, places):
    feats = state.shape[1]
    span = high + 2 * STEPS
    half = span // 2
    odd, core = lax.rem(lax.axis_index("row"), 2), lax.axis_index("col")
    low = lax.broadcasted_iota(jnp.int32, (8, feats + 128), 0) < STEPS
    tiles = []
    for r in range(span):
        if r < high:
            first = [
                jnp.concatenate(
                    [
                        state[r * wide + c : r * wide + c + 8],
                        jnp.broadcast_to(rate[r * wide + c : r * wide + c + 8], (8, 128)),
                    ],
                    axis=1,
                )
                for c in (0, wide - 8)
            ]
        else:
            at = slice((r - high) % STEPS * wide, ((r - high) % STEPS + 1) * wide)
            is_near = (odd == 0) if r < high + STEPS else (odd == 1)
            both = jnp.where(is_near, near[at].astype(F32), far[at].astype(F32))
            first = [both[:8], both[wide - 8 :]]
        tiles.append(jnp.where(low, first[0], first[1]))
    lefts, rights = [], []
    for i in range(half):
        turned = pltpu.roll(tiles[i + half], STEPS, 0)
        lefts.append(jnp.where(low, tiles[i], turned))
        rights.append(jnp.where(low, turned, tiles[i]))
    for i in range(0, half, 2):
        one = jnp.concatenate(lefts[i : i + 2], axis=0)
        two = jnp.concatenate(rights[i : i + 2], axis=0)
        inner[i * 8 : i * 8 + 16] = jnp.where(core == 0, two, one).astype(BF16)
        outer[i * 8 : i * 8 + 16] = jnp.where(core == 0, one, two).astype(BF16)
    count = state.shape[0]
    same = lax.broadcasted_iota(jnp.int32, (count, count), 0) == lax.broadcasted_iota(
        jnp.int32, (count, count), 1
    )
    place = jnp.sum(jnp.where(same, place_row[...], 0).astype(F32), axis=1, keepdims=True)
    hits = lax.broadcasted_iota(jnp.int32, places.shape, 1) == place.astype(jnp.int32)
    places[...] = hits.astype(F32).astype(BF16)


def flow_kernel(wide, high, state, rate, near, far, inner, outer, out, grid, rates):
    feats = state.shape[1]
    span, across = high + 2 * STEPS, wide + 2 * STEPS
    half = span // 2
    odd, core = lax.rem(lax.axis_index("row"), 2), lax.axis_index("col")
    at = lax.broadcasted_iota(jnp.int32, (8, feats + 128), 0)
    low = jnp.where(core == 0, at, 7 - at) < STEPS
    ones, twos = inner[...].astype(F32), outer[...].astype(F32)
    for i in range(half):
        one, two = ones[i * 8 : i * 8 + 8], twos[i * 8 : i * 8 + 8]
        this = jnp.where(low, one, two)
        that = pltpu.roll(jnp.where(low, two, one), STEPS, 0)
        for r, tile in ((i, this), (i + half, that)):
            grid[0, r, wide:] = tile[:, :feats]
            rates[r, wide:] = tile[:, feats:]
    for r in range(high):
        grid[0, r, :wide] = state[r * wide : (r + 1) * wide]
        rates[r, :wide] = jnp.broadcast_to(rate[r * wide : (r + 1) * wide], (wide, 128))
    for at in range(STEPS):
        for ref, start in ((near, high + STEPS * odd), (far, high + STEPS * (1 - odd))):
            strip = ref[at * wide : (at + 1) * wide].astype(F32)
            grid[0, start + at, :wide] = strip[:, :feats]
            rates[start + at, :wide] = strip[:, feats:]
    for step in range(STEPS):
        now, later = step % 2, (step + 1) % 2
        margin = STEPS - 1 - step
        for r in [r % span for r in range(-margin, high + margin)]:
            here = grid[now, r]
            beside = (
                grid[now, (r - 1) % span]
                + grid[now, (r + 1) % span]
                + pltpu.roll(here, 1, 0)
                + pltpu.roll(here, across - 1, 0)
            )
            amount = rates[r]
            amount = jnp.concatenate([amount] * (feats // 128), axis=1)
            here = here + amount * (beside - 4.0 * here)
            if step == STEPS - 1:
                out[r * wide : (r + 1) * wide] = here[:wide]
            else:
                grid[later, r] = here


def physics_kernel(chunk, w_in, w_out, back, act_out, dpre_out):
    feats, hidden = w_in.shape
    cols = chunk[:, :feats]
    dtend = (0.5 * chunk[:, feats:].astype(F32)).astype(BF16)
    tend = adjoint = None
    piece = hidden
    for h in range(0, hidden, piece):
        win, wout = w_in[:, h : h + piece], w_out[:, h : h + piece]
        pre = nn(cols, win)
        dact = nn(dtend, wout)
        sigma = 1.0 / (1.0 + jnp.exp(-pre))
        act = (pre * sigma).astype(BF16)
        dpre = (dact * (sigma * (1.0 + pre * (1.0 - sigma)))).astype(BF16)
        act_out[:, h : h + piece] = act
        dpre_out[:, h : h + piece] = dpre
        tend_h, adj_h = nt(act, wout), nt(dpre, win)
        tend = tend_h if tend is None else tend + tend_h
        adjoint = adj_h if adjoint is None else adjoint + adj_h
    back[:, :feats] = tend.astype(BF16)
    back[:, feats:] = adjoint.astype(BF16)


def hold_kernel(back, out):
    out[...] = back[...]


def grads_of(chunks, acts, dpres, h, piece, feats):
    dpre = jnp.concatenate([d[:, h : h + piece] for d in dpres], axis=0)
    act = jnp.concatenate([a[:, h : h + piece] for a in acts], axis=0)
    return dpre, act


def grads_kernel(owners, *refs):
    chunks, acts, dpres = refs[:owners], refs[owners : 2 * owners], refs[2 * owners : 3 * owners]
    keep, send = refs[3 * owners :]
    feats = chunks[0].shape[1] // 2
    hidden = acts[0].shape[1]
    block = keep.shape[2]
    cols = jnp.concatenate([c[:, :feats] for c in chunks], axis=0).T
    cots = jnp.concatenate([c[:, feats:] for c in chunks], axis=0)
    dtend = (0.5 * cots.astype(F32)).astype(BF16).T
    core = lax.axis_index("col")
    piece = 512
    for h in range(0, hidden, piece):
        dpre, act = grads_of(chunks, acts, dpres, h, piece, feats)
        for which, total in ((0, nn(cols, dpre)), (1, nn(dtend, act))):
            for x in range(2):
                one = total[2 * x * block : (2 * x + 1) * block]
                two = total[(2 * x + 1) * block : (2 * x + 2) * block]
                keep[which, x, :, h : h + piece] = jnp.where(core == 0, one, two)
                send[which, x, :, h : h + piece] = jnp.where(core == 0, two, one).astype(BF16)


def whole_grads_kernel(owners, *refs):
    chunks, acts, dpres = refs[:owners], refs[owners : 2 * owners], refs[2 * owners : 3 * owners]
    out = refs[3 * owners]
    feats = chunks[0].shape[1] // 2
    cols = jnp.concatenate([c[:, :feats] for c in chunks], axis=0).T
    cots = jnp.concatenate([c[:, feats:] for c in chunks], axis=0)
    dtend = (0.5 * cots.astype(F32)).astype(BF16).T
    piece = 256
    for h in range(0, acts[0].shape[1], piece):
        dpre, act = grads_of(chunks, acts, dpres, h, piece, feats)
        out[:feats, h : h + piece] = nn(cols, dpre)
        out[feats:, h : h + piece] = nn(dtend, act)


def gap_kernel(out):
    out[...] = jnp.zeros_like(out)


def share_kernel(keep, got, mine, *sends):
    row = lax.axis_index("row")
    y, x = lax.div(row, 2), lax.rem(row, 2)
    mine[...] = keep[y, x] + got[y, x].astype(F32)
    for send, (dy, dx) in zip(sends, ((1, 1), (0, 1), (1, 0))):
        send[...] = (keep[y ^ dy, x ^ dx] + got[y ^ dy, x ^ dx].astype(F32)).astype(BF16)


def gather_kernel(mine, one, two, three, out):
    rows, hidden = mine.shape
    for j in range(hidden // 128):
        at = slice(j * 128, (j + 1) * 128)
        total = mine[:, at] + one[:, at].astype(F32) + (two[:, at].astype(F32) + three[:, at].astype(F32))
        out[pl.ds(j, rows, stride=hidden // 128), :] = total


def finish_kernel(owners, field, places, *refs):
    backs, new_state, column_adjoint = refs[:owners], refs[owners], refs[owners + 1]
    feats = field.shape[1]
    cap = backs[0].shape[0]
    rows = nn(places[...], jnp.concatenate([b[...] for b in backs], axis=0))
    new_state[...] = field[...] + 0.5 * rows[:, :feats]
    column_adjoint[...] = rows[:, feats:].astype(BF16)


def swap(axis, bit):
    return [(i, i ^ bit) for i in range(lax.axis_size(axis))]


def partners(k):
    owners, cores = lax.axis_size("grp"), lax.axis_size("col")
    pairs = [(g * cores, (g - k) % owners * cores + 1) for g in range(owners)]
    return pairs + [(b, a) for a, b in pairs]


def outward(axis):
    count = lax.axis_size(axis)
    return [(i, (i + 2 * (i % 2) - 1) % count) for i in range(count)]


def local(state, rate, cotangent, dest, w_in, w_out):
    high, wide, feats = state.shape
    count = high * wide
    owners = lax.axis_size("grp")
    cap = 2 * count // owners
    hidden = w_in.shape[2]
    flat_state = state.reshape(count, feats)
    flat_cot = cotangent.reshape(count, feats)

    weight = shape((feats, hidden), BF16)
    strip = shape((STEPS * wide, feats + 128), BF16)
    *chunks, inner, outer, rate_col, place_row, weight_in, weight_out = call(
        functools.partial(pack_kernel, owners, cap, wide, high),
        [dest.reshape(1, count), rate, flat_state, flat_cot, w_in[0], w_out[0]],
        [shape((cap, 2 * feats), BF16)] * owners
        + [strip, strip, shape((count, 1), F32), shape((1, count), jnp.int32), weight, weight],
        [
            pltpu.VMEM((1, count), jnp.int32),
            pltpu.VMEM((high, wide), F32),
            pltpu.VMEM((count, feats), F32),
            pltpu.VMEM((count, feats), BF16),
            pltpu.SemaphoreType.DMA((6,)),
        ],
        far=(0, 1, 2, 3, 4, 5),
    )
    got = [chunks[0]] + [None] * (owners - 1)
    for k in range(owners - 1, 0, -1):
        got[k] = lax.ppermute(chunks[k], ("grp", "col"), partners(k))
    far = lax.ppermute(outer, "row", outward("row"))
    near = lax.ppermute(inner, "row", swap("row", 1))

    backs, acts, dpres = [None] * owners, [None] * owners, [None] * owners

    def physics(k, after=(), held=False):
        made = [shape((cap, 2 * feats), BF16)] + [shape((cap, hidden), BF16)] * 2
        backs[k], acts[k], dpres[k] = call(
            physics_kernel, [got[k], weight_in, weight_out], made, after=after
        )
        if k > 0 and not held:
            backs[k] = lax.ppermute(backs[k], ("grp", "col"), partners(k))
        return (acts[k],)

    physics(0)
    done = (acts[0],)
    done = physics(3, done, True)
    side = shape(((high + 2 * STEPS) * STEPS, feats + 128), BF16)
    inner, outer, places = call(
        functools.partial(edge_kernel, wide, high),
        [flat_state, rate_col, near, far, place_row],
        [side, side, shape((count, owners * cap), BF16)],
        after=done,
    )
    outer_back = lax.ppermute(outer, ("grp", "col"), outward(("grp", "col")))
    inner_back = lax.ppermute(inner, "col", swap("col", 1))
    done = (places,)
    (back,) = call(hold_kernel, [backs[3]], [shape(backs[3].shape, BF16)], after=(places,))
    backs[3] = lax.ppermute(back, ("grp", "col"), partners(3))
    done = physics(2, done)
    done = physics(1, done)
    for k in range(4, owners):
        done = physics(k, done)

    parts = lax.axis_size("row") * lax.axis_size("col")
    block = 2 * feats // parts
    if lax.axis_size("row") == 4 and lax.axis_size("col") == 2:
        keep, send = call(
            functools.partial(grads_kernel, owners),
            [*got, *acts, *dpres],
            [shape((2, 2, block, hidden), F32), shape((2, 2, block, hidden), BF16)],
        )
        arrived = lax.ppermute(send, "col", swap("col", 1))
        (gap,) = call(gap_kernel, [], [shape((8, 128), F32)], after=(keep,), flops=10000000000)
        mine, *shares = call(
            share_kernel,
            [keep, arrived],
            [shape((block, hidden), F32)] + [shape((block, hidden), BF16)] * 3,
            after=(gap,),
        )
        done = (mine,)
        shares = [lax.ppermute(s, "row", swap("row", bit)) for bit, s in zip((3, 1, 2), shares)]
        (summed,) = call(
            gather_kernel, [mine, *shares], [shape((block * hidden // 128, 128), F32)]
        )
    else:
        (flat,) = call(
            functools.partial(whole_grads_kernel, owners),
            [*got, *acts, *dpres],
            [shape((2 * feats, hidden), F32)],
        )
        done = (flat,)
        summed = lax.psum_scatter(
            flat.reshape(-1, 128), ("row", "col"), scatter_dimension=0, tiled=True
        )
    (field,) = call(
        functools.partial(flow_kernel, wide, high),
        [flat_state, rate_col, near, far, inner_back, outer_back],
        [shape((count, feats), F32)],
        [
            pltpu.VMEM((2, high + 2 * STEPS, wide + 2 * STEPS, feats), F32),
            pltpu.VMEM((high + 2 * STEPS, wide + 2 * STEPS, 128), F32),
        ],
        after=done,
    )
    new_state, column_adjoint = call(
        functools.partial(finish_kernel, owners),
        [field, places, *backs],
        [shape((count, feats), F32), shape((count, feats), BF16)],
    )
    return (
        new_state.reshape(state.shape),
        column_adjoint.reshape(state.shape),
        summed[None],
    )


def solution(mesh):
    in_specs = (
        P("row", ("grp", "col"), None),
        P("row", ("grp", "col")),
        P("row", ("grp", "col"), None),
        P("row", ("grp", "col"), None, None),
        P("grp", None, None),
        P("grp", None, None),
    )
    out_specs = (
        P("row", ("grp", "col"), None),
        P("row", ("grp", "col"), None),
        P("grp", ("row", "col"), None),
    )
    return jax.shard_map(local, mesh=mesh, in_specs=in_specs, out_specs=out_specs, check_vma=False)
```

```python
import functools

import jax
import jax.numpy as jnp
from jax import lax
from jax.experimental import pallas as pl
from jax.experimental.pallas import tpu as pltpu
from jax.sharding import PartitionSpec as P

STEPS = 4
LANES = 32
BF16 = jnp.bfloat16
F32 = jnp.float32
VMEM = pl.BlockSpec(memory_space=pltpu.VMEM)
HBM = pl.BlockSpec(memory_space=pltpu.HBM)
ANY = pl.BlockSpec(memory_space=pl.ANY)


def call(kernel, ins, outs, scratch=(), after=(), far=(), vmem=24 << 20, flops=None):
    ins = [
        pltpu.with_memory_space_constraint(x, pltpu.HBM) if n in far else x
        for n, x in enumerate(ins)
    ]
    specs = [HBM if n in far else VMEM for n in range(len(ins))]
    count = len(ins)

    def body(*refs):
        kernel(*refs[:count], *refs[count + len(after) :])

    return pl.pallas_call(
        body,
        out_shape=list(outs),
        in_specs=specs + [ANY] * len(after),
        out_specs=[VMEM] * len(outs),
        scratch_shapes=list(scratch),
        compiler_params=pltpu.CompilerParams(vmem_limit_bytes=vmem),
        cost_estimate=flops and pl.CostEstimate(flops=flops, bytes_accessed=0, transcendentals=0),
    )(*ins, *after)


def shape(dims, dtype):
    return jax.ShapeDtypeStruct(dims, dtype)


def nt(a, b):
    return lax.dot_general(a, b, (((1,), (1,)), ((), ())), preferred_element_type=F32)


def nn(a, b):
    return jnp.dot(a, b, preferred_element_type=F32)


def sealed(fields, rates):
    cells, feats = fields.shape
    groups = [rates[g : g + 16, :LANES] for g in range(0, cells, 16)]
    rest = jnp.zeros((16, feats - LANES * len(groups)), F32)
    return jnp.concatenate([fields, jnp.concatenate([*groups, rest], axis=1)], axis=0).astype(BF16)


def opened(message):
    rows = message.astype(F32)
    cells = rows.shape[0] - 16
    lanes = range(0, cells // 16 * LANES, LANES)
    rates = [jnp.broadcast_to(rows[cells:, at : at + 1], (16, 128)) for at in lanes]
    return jnp.concatenate([rows[:cells], jnp.concatenate(rates, axis=0)], axis=1)


def pack_kernel(owners, cap, wide, high, *refs):
    far, near, sems = refs[:6], [*refs[-5:-1], *refs[-7:-5]], refs[-1]
    chunks, inner, outer, rate_cols, places = refs[6 : owners + 6], *refs[owners + 6 : -7]
    copies = [pltpu.make_async_copy(a, b, sems.at[n]) for n, (a, b) in enumerate(zip(far, near))]
    for copy in copies:
        copy.start()
    dest, rate, state, cot, _, _ = near
    count, feats = state.shape
    copies[0].wait()
    named = lax.broadcasted_iota(jnp.int32, (max(8, owners), count), 0) == dest[...]
    earlier = lax.broadcasted_iota(jnp.int32, (count, count), 0) < lax.broadcasted_iota(
        jnp.int32, (count, count), 1
    )
    ranks = nn(named.astype(F32).astype(BF16), earlier.astype(F32).astype(BF16))
    slot = jnp.sum(jnp.where(named, ranks, 0.0), axis=0, keepdims=True).astype(jnp.int32)
    ahead = dest[...] - lax.axis_index("grp")
    turn = jnp.where(lax.axis_index("col") == 0, -ahead, ahead)
    place = jnp.where(turn < 0, turn + owners, turn) * cap + slot
    places[...] = place
    for copy in copies[1:4]:
        copy.wait()
    turned = rate[...].T
    for r in range(high):
        rate_cols[r * wide : (r + 1) * wide] = turned[:, r : r + 1]
    cols = state[...].astype(BF16)
    cots = cot[...]
    for k in range(owners):
        rows = lax.broadcasted_iota(jnp.int32, (cap, count), 0) + k * cap
        placing = (rows == place).astype(F32).astype(BF16)
        chunks[k][:, :feats] = nn(placing, cols).astype(BF16)
        chunks[k][:, feats:] = nn(placing, cots).astype(BF16)
    strip = STEPS * wide
    odd = lax.rem(lax.axis_index("row"), 2)
    for out, top in ((inner, odd), (outer, 1 - odd)):
        start = pl.multiple_of((1 - top) * (count - strip), strip)
        cells = pl.ds(start, strip)
        out[...] = sealed(state[cells], jnp.broadcast_to(rate_cols[cells], (strip, 128)))
    for copy in copies[4:]:
        copy.wait()


def edge_kernel(wide, high, state, rate, near, far, place_row, inner, outer, places):
    feats = state.shape[1]
    span = high + 2 * STEPS
    half = span // 2
    odd, core = lax.rem(lax.axis_index("row"), 2), lax.axis_index("col")
    low = lax.broadcasted_iota(jnp.int32, (8, feats + 128), 0) < STEPS
    nears, fars = opened(near[...]), opened(far[...])
    tiles = []
    for r in range(span):
        if r < high:
            first = [
                jnp.concatenate(
                    [
                        state[r * wide + c : r * wide + c + 8],
                        jnp.broadcast_to(rate[r * wide + c : r * wide + c + 8], (8, 128)),
                    ],
                    axis=1,
                )
                for c in (0, wide - 8)
            ]
        else:
            at = slice((r - high) % STEPS * wide, ((r - high) % STEPS + 1) * wide)
            is_near = (odd == 0) if r < high + STEPS else (odd == 1)
            both = jnp.where(is_near, nears[at], fars[at])
            first = [both[:8], both[wide - 8 :]]
        tiles.append(jnp.where(low, first[0], first[1]))
    lefts, rights = [], []
    for i in range(half):
        turned = pltpu.roll(tiles[i + half], STEPS, 0)
        lefts.append(jnp.where(low, tiles[i], turned))
        rights.append(jnp.where(low, turned, tiles[i]))
    one, two = jnp.concatenate(lefts, axis=0), jnp.concatenate(rights, axis=0)
    for out, strip in ((inner, jnp.where(core == 0, two, one)), (outer, jnp.where(core == 0, one, two))):
        out[...] = sealed(strip[:, :feats], strip[:, feats:])
    count = state.shape[0]
    same = lax.broadcasted_iota(jnp.int32, (count, count), 0) == lax.broadcasted_iota(
        jnp.int32, (count, count), 1
    )
    place = jnp.sum(jnp.where(same, place_row[...], 0).astype(F32), axis=1, keepdims=True)
    hits = lax.broadcasted_iota(jnp.int32, places.shape, 1) == place.astype(jnp.int32)
    places[...] = hits.astype(F32).astype(BF16)


def flow_kernel(wide, high, state, rate, near, far, inner, outer, out, grid, rates):
    feats = state.shape[1]
    span, across = high + 2 * STEPS, wide + 2 * STEPS
    half = span // 2
    odd, core = lax.rem(lax.axis_index("row"), 2), lax.axis_index("col")
    at = lax.broadcasted_iota(jnp.int32, (8, feats + 128), 0)
    low = jnp.where(core == 0, at, 7 - at) < STEPS
    ones, twos = opened(inner[...]), opened(outer[...])
    for i in range(half):
        one, two = ones[i * 8 : i * 8 + 8], twos[i * 8 : i * 8 + 8]
        this = jnp.where(low, one, two)
        that = pltpu.roll(jnp.where(low, two, one), STEPS, 0)
        for r, tile in ((i, this), (i + half, that)):
            grid[0, r, wide:] = tile[:, :feats]
            rates[r, wide:] = tile[:, feats:]
    for r in range(high):
        grid[0, r, :wide] = state[r * wide : (r + 1) * wide]
        rates[r, :wide] = jnp.broadcast_to(rate[r * wide : (r + 1) * wide], (wide, 128))
    for ref, start in ((near, high + STEPS * odd), (far, high + STEPS * (1 - odd))):
        cells = opened(ref[...])
        for at in range(STEPS):
            strip = cells[at * wide : (at + 1) * wide]
            grid[0, start + at, :wide] = strip[:, :feats]
            rates[start + at, :wide] = strip[:, feats:]
    for step in range(STEPS):
        now, later = step % 2, (step + 1) % 2
        margin = STEPS - 1 - step
        for r in [r % span for r in range(-margin, high + margin)]:
            here = grid[now, r]
            beside = (
                grid[now, (r - 1) % span]
                + grid[now, (r + 1) % span]
                + pltpu.roll(here, 1, 0)
                + pltpu.roll(here, across - 1, 0)
            )
            amount = rates[r]
            amount = jnp.concatenate([amount] * (feats // 128), axis=1)
            here = here + amount * (beside - 4.0 * here)
            if step == STEPS - 1:
                out[r * wide : (r + 1) * wide] = here[:wide]
            else:
                grid[later, r] = here


def physics_kernel(chunk, w_in, w_out, back, act_out, dpre_out):
    feats, hidden = w_in.shape
    cols = chunk[:, :feats]
    dtend = (0.5 * chunk[:, feats:].astype(F32)).astype(BF16)
    tend = adjoint = None
    piece = hidden
    for h in range(0, hidden, piece):
        win, wout = w_in[:, h : h + piece], w_out[:, h : h + piece]
        pre = nn(cols, win)
        dact = nn(dtend, wout)
        sigma = 1.0 / (1.0 + jnp.exp(-pre))
        act = (pre * sigma).astype(BF16)
        dpre = (dact * (sigma * (1.0 + pre * (1.0 - sigma)))).astype(BF16)
        act_out[:, h : h + piece] = act
        dpre_out[:, h : h + piece] = dpre
        tend_h, adj_h = nt(act, wout), nt(dpre, win)
        tend = tend_h if tend is None else tend + tend_h
        adjoint = adj_h if adjoint is None else adjoint + adj_h
    back[:, :feats] = tend.astype(BF16)
    back[:, feats:] = adjoint.astype(BF16)


def hold_kernel(back, out):
    out[...] = back[...]


def grads_of(chunks, acts, dpres, h, piece, feats):
    dpre = jnp.concatenate([d[:, h : h + piece] for d in dpres], axis=0)
    act = jnp.concatenate([a[:, h : h + piece] for a in acts], axis=0)
    return dpre, act


def grads_kernel(owners, *refs):
    chunks, acts, dpres = refs[:owners], refs[owners : 2 * owners], refs[2 * owners : 3 * owners]
    keep, send = refs[3 * owners :]
    feats = chunks[0].shape[1] // 2
    hidden = acts[0].shape[1]
    block = keep.shape[2]
    cols = jnp.concatenate([c[:, :feats] for c in chunks], axis=0).T
    cots = jnp.concatenate([c[:, feats:] for c in chunks], axis=0)
    dtend = (0.5 * cots.astype(F32)).astype(BF16).T
    core = lax.axis_index("col")
    piece = 512
    for h in range(0, hidden, piece):
        dpre, act = grads_of(chunks, acts, dpres, h, piece, feats)
        for which, total in ((0, nn(cols, dpre)), (1, nn(dtend, act))):
            for x in range(2):
                one = total[2 * x * block : (2 * x + 1) * block]
                two = total[(2 * x + 1) * block : (2 * x + 2) * block]
                keep[which, x, :, h : h + piece] = jnp.where(core == 0, one, two)
                send[which, x, :, h : h + piece] = jnp.where(core == 0, two, one).astype(BF16)


def whole_grads_kernel(owners, *refs):
    chunks, acts, dpres = refs[:owners], refs[owners : 2 * owners], refs[2 * owners : 3 * owners]
    out = refs[3 * owners]
    feats = chunks[0].shape[1] // 2
    cols = jnp.concatenate([c[:, :feats] for c in chunks], axis=0).T
    cots = jnp.concatenate([c[:, feats:] for c in chunks], axis=0)
    dtend = (0.5 * cots.astype(F32)).astype(BF16).T
    piece = 256
    for h in range(0, acts[0].shape[1], piece):
        dpre, act = grads_of(chunks, acts, dpres, h, piece, feats)
        out[:feats, h : h + piece] = nn(cols, dpre)
        out[feats:, h : h + piece] = nn(dtend, act)


def gap_kernel(out):
    out[...] = jnp.zeros_like(out)


def share_kernel(keep, got, mine, *sends):
    row = lax.axis_index("row")
    y, x = lax.div(row, 2), lax.rem(row, 2)
    mine[...] = keep[y, x] + got[y, x].astype(F32)
    for send, (dy, dx) in zip(sends, ((1, 1), (0, 1), (1, 0))):
        send[...] = (keep[y ^ dy, x ^ dx] + got[y ^ dy, x ^ dx].astype(F32)).astype(BF16)


def gather_kernel(mine, one, two, three, out):
    rows, hidden = mine.shape
    for j in range(hidden // 128):
        at = slice(j * 128, (j + 1) * 128)
        total = mine[:, at] + one[:, at].astype(F32) + (two[:, at].astype(F32) + three[:, at].astype(F32))
        out[pl.ds(j, rows, stride=hidden // 128), :] = total


def finish_kernel(owners, field, places, *refs):
    backs, new_state, column_adjoint = refs[:owners], refs[owners], refs[owners + 1]
    feats = field.shape[1]
    cap = backs[0].shape[0]
    rows = nn(places[...], jnp.concatenate([b[...] for b in backs], axis=0))
    new_state[...] = field[...] + 0.5 * rows[:, :feats]
    column_adjoint[...] = rows[:, feats:].astype(BF16)


def swap(axis, bit):
    return [(i, i ^ bit) for i in range(lax.axis_size(axis))]


def partners(k):
    owners, cores = lax.axis_size("grp"), lax.axis_size("col")
    pairs = [(g * cores, (g - k) % owners * cores + 1) for g in range(owners)]
    return pairs + [(b, a) for a, b in pairs]


def outward(axis):
    count = lax.axis_size(axis)
    return [(i, (i + 2 * (i % 2) - 1) % count) for i in range(count)]


def local(state, rate, cotangent, dest, w_in, w_out):
    high, wide, feats = state.shape
    count = high * wide
    owners = lax.axis_size("grp")
    cap = 2 * count // owners
    hidden = w_in.shape[2]
    flat_state = state.reshape(count, feats)
    flat_cot = cotangent.reshape(count, feats)

    weight = shape((feats, hidden), BF16)
    strip = shape((STEPS * wide + 16, feats), BF16)
    *chunks, inner, outer, rate_col, place_row, weight_in, weight_out = call(
        functools.partial(pack_kernel, owners, cap, wide, high),
        [dest.reshape(1, count), rate, flat_state, flat_cot, w_in[0], w_out[0]],
        [shape((cap, 2 * feats), BF16)] * owners
        + [strip, strip, shape((count, 1), F32), shape((1, count), jnp.int32), weight, weight],
        [
            pltpu.VMEM((1, count), jnp.int32),
            pltpu.VMEM((high, wide), F32),
            pltpu.VMEM((count, feats), F32),
            pltpu.VMEM((count, feats), BF16),
            pltpu.SemaphoreType.DMA((6,)),
        ],
        far=(0, 1, 2, 3, 4, 5),
    )
    got = [chunks[0]] + [None] * (owners - 1)
    for k in range(owners - 1, 0, -1):
        got[k] = lax.ppermute(chunks[k], ("grp", "col"), partners(k))
    far = lax.ppermute(outer, "row", outward("row"))
    near = lax.ppermute(inner, "row", swap("row", 1))

    backs, acts, dpres = [None] * owners, [None] * owners, [None] * owners

    def physics(k, after=(), held=False):
        made = [shape((cap, 2 * feats), BF16)] + [shape((cap, hidden), BF16)] * 2
        backs[k], acts[k], dpres[k] = call(
            physics_kernel, [got[k], weight_in, weight_out], made, after=after
        )
        if k > 0 and not held:
            backs[k] = lax.ppermute(backs[k], ("grp", "col"), partners(k))
        return (acts[k],)

    physics(0)
    done = (acts[0],)
    done = physics(3, done, True)
    side = shape(((high + 2 * STEPS) * STEPS + 16, feats), BF16)
    inner, outer, places = call(
        functools.partial(edge_kernel, wide, high),
        [flat_state, rate_col, near, far, place_row],
        [side, side, shape((count, owners * cap), BF16)],
        after=done,
    )
    outer_back = lax.ppermute(outer, ("grp", "col"), outward(("grp", "col")))
    inner_back = lax.ppermute(inner, "col", swap("col", 1))
    done = (places,)
    (back,) = call(hold_kernel, [backs[3]], [shape(backs[3].shape, BF16)], after=(places,))
    backs[3] = lax.ppermute(back, ("grp", "col"), partners(3))
    done = physics(2, done)
    done = physics(1, done)
    for k in range(4, owners):
        done = physics(k, done)

    parts = lax.axis_size("row") * lax.axis_size("col")
    block = 2 * feats // parts
    if lax.axis_size("row") == 4 and lax.axis_size("col") == 2:
        keep, send = call(
            functools.partial(grads_kernel, owners),
            [*got, *acts, *dpres],
            [shape((2, 2, block, hidden), F32), shape((2, 2, block, hidden), BF16)],
        )
        arrived = lax.ppermute(send, "col", swap("col", 1))
        (gap,) = call(gap_kernel, [], [shape((8, 128), F32)], after=(keep,), flops=10000000000)
        mine, *shares = call(
            share_kernel,
            [keep, arrived],
            [shape((block, hidden), F32)] + [shape((block, hidden), BF16)] * 3,
            after=(gap,),
        )
        done = (mine,)
        shares = [lax.ppermute(s, "row", swap("row", bit)) for bit, s in zip((3, 1, 2), shares)]
        (summed,) = call(
            gather_kernel, [mine, *shares], [shape((block * hidden // 128, 128), F32)]
        )
    else:
        (flat,) = call(
            functools.partial(whole_grads_kernel, owners),
            [*got, *acts, *dpres],
            [shape((2 * feats, hidden), F32)],
        )
        done = (flat,)
        summed = lax.psum_scatter(
            flat.reshape(-1, 128), ("row", "col"), scatter_dimension=0, tiled=True
        )
    (field,) = call(
        functools.partial(flow_kernel, wide, high),
        [flat_state, rate_col, near, far, inner_back, outer_back],
        [shape((count, feats), F32)],
        [
            pltpu.VMEM((2, high + 2 * STEPS, wide + 2 * STEPS, feats), F32),
            pltpu.VMEM((high + 2 * STEPS, wide + 2 * STEPS, 128), F32),
        ],
        after=done,
    )
    new_state, column_adjoint = call(
        functools.partial(finish_kernel, owners),
        [field, places, *backs],
        [shape((count, feats), F32), shape((count, feats), BF16)],
    )
    return (
        new_state.reshape(state.shape),
        column_adjoint.reshape(state.shape),
        summed[None],
    )


def solution(mesh):
    in_specs = (
        P("row", ("grp", "col"), None),
        P("row", ("grp", "col")),
        P("row", ("grp", "col"), None),
        P("row", ("grp", "col"), None, None),
        P("grp", None, None),
        P("grp", None, None),
    )
    out_specs = (
        P("row", ("grp", "col"), None),
        P("row", ("grp", "col"), None),
        P("grp", ("row", "col"), None),
    )
    return jax.shard_map(local, mesh=mesh, in_specs=in_specs, out_specs=out_specs, check_vma=False)
```

```python
import functools

import jax
import jax.numpy as jnp
from jax import lax
from jax.experimental import pallas as pl
from jax.experimental.pallas import tpu as pltpu
from jax.sharding import PartitionSpec as P

STEPS = 4
LANES = 32
BF16 = jnp.bfloat16
F32 = jnp.float32
VMEM = pl.BlockSpec(memory_space=pltpu.VMEM)
HBM = pl.BlockSpec(memory_space=pltpu.HBM)
ANY = pl.BlockSpec(memory_space=pl.ANY)


def call(kernel, ins, outs, scratch=(), after=(), far=(), vmem=24 << 20, flops=None):
    ins = [
        pltpu.with_memory_space_constraint(x, pltpu.HBM) if n in far else x
        for n, x in enumerate(ins)
    ]
    specs = [HBM if n in far else VMEM for n in range(len(ins))]
    count = len(ins)

    def body(*refs):
        kernel(*refs[:count], *refs[count + len(after) :])

    return pl.pallas_call(
        body,
        out_shape=list(outs),
        in_specs=specs + [ANY] * len(after),
        out_specs=[VMEM] * len(outs),
        scratch_shapes=list(scratch),
        compiler_params=pltpu.CompilerParams(vmem_limit_bytes=vmem),
        cost_estimate=flops and pl.CostEstimate(flops=flops, bytes_accessed=0, transcendentals=0),
    )(*ins, *after)


def shape(dims, dtype):
    return jax.ShapeDtypeStruct(dims, dtype)


def nt(a, b):
    return lax.dot_general(a, b, (((1,), (1,)), ((), ())), preferred_element_type=F32)


def nn(a, b):
    return jnp.dot(a, b, preferred_element_type=F32)


def sealed(fields, rates):
    cells, feats = fields.shape
    groups = [rates[g : g + 16, :LANES] for g in range(0, cells, 16)]
    rest = jnp.zeros((16, feats - LANES * len(groups)), F32)
    return jnp.concatenate([fields, jnp.concatenate([*groups, rest], axis=1)], axis=0).astype(BF16)


def opened(message):
    rows = message.astype(F32)
    cells = rows.shape[0] - 16
    lanes = range(0, cells // 16 * LANES, LANES)
    rates = [jnp.broadcast_to(rows[cells:, at : at + 1], (16, 128)) for at in lanes]
    return jnp.concatenate([rows[:cells], jnp.concatenate(rates, axis=0)], axis=1)


def pack_kernel(owners, cap, wide, high, *refs):
    far, near, sems = refs[:6], [*refs[-5:-1], *refs[-7:-5]], refs[-1]
    chunks, inner, outer, rate_cols, places = refs[6 : owners + 6], *refs[owners + 6 : -7]
    copies = [pltpu.make_async_copy(a, b, sems.at[n]) for n, (a, b) in enumerate(zip(far, near))]
    for copy in copies:
        copy.start()
    dest, rate, state, cot, _, _ = near
    count, feats = state.shape
    copies[0].wait()
    named = lax.broadcasted_iota(jnp.int32, (max(8, owners), count), 0) == dest[...]
    earlier = lax.broadcasted_iota(jnp.int32, (count, count), 0) < lax.broadcasted_iota(
        jnp.int32, (count, count), 1
    )
    ranks = nn(named.astype(F32).astype(BF16), earlier.astype(F32).astype(BF16))
    slot = jnp.sum(jnp.where(named, ranks, 0.0), axis=0, keepdims=True).astype(jnp.int32)
    ahead = dest[...] - lax.axis_index("grp")
    turn = jnp.where(lax.axis_index("col") == 0, -ahead, ahead)
    place = jnp.where(turn < 0, turn + owners, turn) * cap + slot
    places[...] = place
    for copy in copies[1:4]:
        copy.wait()
    turned = rate[...].T
    for r in range(high):
        rate_cols[r * wide : (r + 1) * wide] = turned[:, r : r + 1]
    cols = state[...].astype(BF16)
    cots = cot[...]
    for k in range(owners):
        rows = lax.broadcasted_iota(jnp.int32, (cap, count), 0) + k * cap
        placing = (rows == place).astype(F32).astype(BF16)
        chunks[k][:, :feats] = nn(placing, cols).astype(BF16)
        chunks[k][:, feats:] = nn(placing, cots).astype(BF16)
    strip = STEPS * wide
    odd = lax.rem(lax.axis_index("row"), 2)
    for out, top in ((inner, odd), (outer, 1 - odd)):
        start = pl.multiple_of((1 - top) * (count - strip), strip)
        cells = pl.ds(start, strip)
        out[...] = sealed(state[cells], jnp.broadcast_to(rate_cols[cells], (strip, 128)))
    for copy in copies[4:]:
        copy.wait()


def edge_kernel(wide, high, state, rate, near, far, inner, outer):
    feats = state.shape[1]
    span = high + 2 * STEPS
    half = span // 2
    odd, core = lax.rem(lax.axis_index("row"), 2), lax.axis_index("col")
    low = lax.broadcasted_iota(jnp.int32, (8, feats + 128), 0) < STEPS
    nears, fars = opened(near[...]), opened(far[...])
    tiles = []
    for r in range(span):
        if r < high:
            first = [
                jnp.concatenate(
                    [
                        state[r * wide + c : r * wide + c + 8],
                        jnp.broadcast_to(rate[r * wide + c : r * wide + c + 8], (8, 128)),
                    ],
                    axis=1,
                )
                for c in (0, wide - 8)
            ]
        else:
            at = slice((r - high) % STEPS * wide, ((r - high) % STEPS + 1) * wide)
            is_near = (odd == 0) if r < high + STEPS else (odd == 1)
            both = jnp.where(is_near, nears[at], fars[at])
            first = [both[:8], both[wide - 8 :]]
        tiles.append(jnp.where(low, first[0], first[1]))
    lefts, rights = [], []
    for i in range(half):
        turned = pltpu.roll(tiles[i + half], STEPS, 0)
        lefts.append(jnp.where(low, tiles[i], turned))
        rights.append(jnp.where(low, turned, tiles[i]))
    one, two = jnp.concatenate(lefts, axis=0), jnp.concatenate(rights, axis=0)
    for out, strip in ((inner, jnp.where(core == 0, two, one)), (outer, jnp.where(core == 0, one, two))):
        out[...] = sealed(strip[:, :feats], strip[:, feats:])


def flow_kernel(wide, high, state, rate, near, far, inner, outer, place_row, out, places, grid, rates):
    count = state.shape[0]
    same = lax.broadcasted_iota(jnp.int32, (count, count), 0) == lax.broadcasted_iota(
        jnp.int32, (count, count), 1
    )
    place = jnp.sum(jnp.where(same, place_row[...], 0).astype(F32), axis=1, keepdims=True)
    hits = lax.broadcasted_iota(jnp.int32, places.shape, 1) == place.astype(jnp.int32)
    places[...] = hits.astype(F32).astype(BF16)
    feats = state.shape[1]
    span, across = high + 2 * STEPS, wide + 2 * STEPS
    half = span // 2
    odd, core = lax.rem(lax.axis_index("row"), 2), lax.axis_index("col")
    at = lax.broadcasted_iota(jnp.int32, (8, feats + 128), 0)
    low = jnp.where(core == 0, at, 7 - at) < STEPS
    ones, twos = opened(inner[...]), opened(outer[...])
    for i in range(half):
        one, two = ones[i * 8 : i * 8 + 8], twos[i * 8 : i * 8 + 8]
        this = jnp.where(low, one, two)
        that = pltpu.roll(jnp.where(low, two, one), STEPS, 0)
        for r, tile in ((i, this), (i + half, that)):
            grid[0, r, wide:] = tile[:, :feats]
            rates[r, wide:] = tile[:, feats:]
    for r in range(high):
        grid[0, r, :wide] = state[r * wide : (r + 1) * wide]
        rates[r, :wide] = jnp.broadcast_to(rate[r * wide : (r + 1) * wide], (wide, 128))
    for ref, start in ((near, high + STEPS * odd), (far, high + STEPS * (1 - odd))):
        cells = opened(ref[...])
        for at in range(STEPS):
            strip = cells[at * wide : (at + 1) * wide]
            grid[0, start + at, :wide] = strip[:, :feats]
            rates[start + at, :wide] = strip[:, feats:]
    for step in range(STEPS):
        now, later = step % 2, (step + 1) % 2
        margin = STEPS - 1 - step
        for r in [r % span for r in range(-margin, high + margin)]:
            here = grid[now, r]
            beside = (
                grid[now, (r - 1) % span]
                + grid[now, (r + 1) % span]
                + pltpu.roll(here, 1, 0)
                + pltpu.roll(here, across - 1, 0)
            )
            amount = rates[r]
            amount = jnp.concatenate([amount] * (feats // 128), axis=1)
            here = here + amount * (beside - 4.0 * here)
            if step == STEPS - 1:
                out[r * wide : (r + 1) * wide] = here[:wide]
            else:
                grid[later, r] = here


def physics_kernel(chunk, w_in, w_out, back, act_out, dpre_out):
    feats, hidden = w_in.shape
    cols = chunk[:, :feats]
    dtend = (0.5 * chunk[:, feats:].astype(F32)).astype(BF16)
    tend = adjoint = None
    piece = hidden
    for h in range(0, hidden, piece):
        win, wout = w_in[:, h : h + piece], w_out[:, h : h + piece]
        pre = nn(cols, win)
        dact = nn(dtend, wout)
        sigma = 1.0 / (1.0 + jnp.exp(-pre))
        act = (pre * sigma).astype(BF16)
        dpre = (dact * (sigma * (1.0 + pre * (1.0 - sigma)))).astype(BF16)
        act_out[:, h : h + piece] = act
        dpre_out[:, h : h + piece] = dpre
        tend_h, adj_h = nt(act, wout), nt(dpre, win)
        tend = tend_h if tend is None else tend + tend_h
        adjoint = adj_h if adjoint is None else adjoint + adj_h
    back[:, :feats] = tend.astype(BF16)
    back[:, feats:] = adjoint.astype(BF16)


def hold_kernel(back, out):
    out[...] = back[...]


def grads_of(chunks, acts, dpres, h, piece, feats):
    dpre = jnp.concatenate([d[:, h : h + piece] for d in dpres], axis=0)
    act = jnp.concatenate([a[:, h : h + piece] for a in acts], axis=0)
    return dpre, act


def grads_kernel(owners, *refs):
    chunks, acts, dpres = refs[:owners], refs[owners : 2 * owners], refs[2 * owners : 3 * owners]
    keep, send = refs[3 * owners :]
    feats = chunks[0].shape[1] // 2
    hidden = acts[0].shape[1]
    block = keep.shape[2]
    cols = jnp.concatenate([c[:, :feats] for c in chunks], axis=0).T
    cots = jnp.concatenate([c[:, feats:] for c in chunks], axis=0)
    dtend = (0.5 * cots.astype(F32)).astype(BF16).T
    core = lax.axis_index("col")
    piece = 512
    for h in range(0, hidden, piece):
        dpre, act = grads_of(chunks, acts, dpres, h, piece, feats)
        for which, total in ((0, nn(cols, dpre)), (1, nn(dtend, act))):
            for x in range(2):
                one = total[2 * x * block : (2 * x + 1) * block]
                two = total[(2 * x + 1) * block : (2 * x + 2) * block]
                keep[which, x, :, h : h + piece] = jnp.where(core == 0, one, two)
                send[which, x, :, h : h + piece] = jnp.where(core == 0, two, one).astype(BF16)


def whole_grads_kernel(owners, *refs):
    chunks, acts, dpres = refs[:owners], refs[owners : 2 * owners], refs[2 * owners : 3 * owners]
    out = refs[3 * owners]
    feats = chunks[0].shape[1] // 2
    cols = jnp.concatenate([c[:, :feats] for c in chunks], axis=0).T
    cots = jnp.concatenate([c[:, feats:] for c in chunks], axis=0)
    dtend = (0.5 * cots.astype(F32)).astype(BF16).T
    piece = 256
    for h in range(0, acts[0].shape[1], piece):
        dpre, act = grads_of(chunks, acts, dpres, h, piece, feats)
        out[:feats, h : h + piece] = nn(cols, dpre)
        out[feats:, h : h + piece] = nn(dtend, act)


def gap_kernel(out):
    out[...] = jnp.zeros_like(out)


def share_kernel(keep, got, mine, *sends):
    row = lax.axis_index("row")
    y, x = lax.div(row, 2), lax.rem(row, 2)
    mine[...] = keep[y, x] + got[y, x].astype(F32)
    for send, (dy, dx) in zip(sends, ((1, 1), (0, 1), (1, 0))):
        send[...] = (keep[y ^ dy, x ^ dx] + got[y ^ dy, x ^ dx].astype(F32)).astype(BF16)


def gather_kernel(mine, one, two, three, out):
    rows, hidden = mine.shape
    for j in range(hidden // 128):
        at = slice(j * 128, (j + 1) * 128)
        total = mine[:, at] + one[:, at].astype(F32) + (two[:, at].astype(F32) + three[:, at].astype(F32))
        out[pl.ds(j, rows, stride=hidden // 128), :] = total


def finish_kernel(owners, field, places, *refs):
    backs, new_state, column_adjoint = refs[:owners], refs[owners], refs[owners + 1]
    feats = field.shape[1]
    cap = backs[0].shape[0]
    rows = nn(places[...], jnp.concatenate([b[...] for b in backs], axis=0))
    new_state[...] = field[...] + 0.5 * rows[:, :feats]
    column_adjoint[...] = rows[:, feats:].astype(BF16)


def swap(axis, bit):
    return [(i, i ^ bit) for i in range(lax.axis_size(axis))]


def partners(k):
    owners, cores = lax.axis_size("grp"), lax.axis_size("col")
    pairs = [(g * cores, (g - k) % owners * cores + 1) for g in range(owners)]
    return pairs + [(b, a) for a, b in pairs]


def outward(axis):
    count = lax.axis_size(axis)
    return [(i, (i + 2 * (i % 2) - 1) % count) for i in range(count)]


def local(state, rate, cotangent, dest, w_in, w_out):
    high, wide, feats = state.shape
    count = high * wide
    owners = lax.axis_size("grp")
    cap = 2 * count // owners
    hidden = w_in.shape[2]
    flat_state = state.reshape(count, feats)
    flat_cot = cotangent.reshape(count, feats)

    weight = shape((feats, hidden), BF16)
    strip = shape((STEPS * wide + 16, feats), BF16)
    *chunks, inner, outer, rate_col, place_row, weight_in, weight_out = call(
        functools.partial(pack_kernel, owners, cap, wide, high),
        [dest.reshape(1, count), rate, flat_state, flat_cot, w_in[0], w_out[0]],
        [shape((cap, 2 * feats), BF16)] * owners
        + [strip, strip, shape((count, 1), F32), shape((1, count), jnp.int32), weight, weight],
        [
            pltpu.VMEM((1, count), jnp.int32),
            pltpu.VMEM((high, wide), F32),
            pltpu.VMEM((count, feats), F32),
            pltpu.VMEM((count, feats), BF16),
            pltpu.SemaphoreType.DMA((6,)),
        ],
        far=(0, 1, 2, 3, 4, 5),
    )
    got = [chunks[0]] + [None] * (owners - 1)
    for k in range(owners - 1, 0, -1):
        got[k] = lax.ppermute(chunks[k], ("grp", "col"), partners(k))
    far = lax.ppermute(outer, "row", outward("row"))
    near = lax.ppermute(inner, "row", swap("row", 1))

    backs, acts, dpres = [None] * owners, [None] * owners, [None] * owners

    def physics(k, after=(), held=False):
        made = [shape((cap, 2 * feats), BF16)] + [shape((cap, hidden), BF16)] * 2
        backs[k], acts[k], dpres[k] = call(
            physics_kernel, [got[k], weight_in, weight_out], made, after=after
        )
        if k > 0 and not held:
            backs[k] = lax.ppermute(backs[k], ("grp", "col"), partners(k))
        return (acts[k],)

    physics(0)
    done = (acts[0],)
    done = physics(3, done, True)
    side = shape(((high + 2 * STEPS) * STEPS + 16, feats), BF16)
    inner, outer = call(
        functools.partial(edge_kernel, wide, high),
        [flat_state, rate_col, near, far],
        [side, side],
        after=done,
    )
    outer_back = lax.ppermute(outer, ("grp", "col"), outward(("grp", "col")))
    inner_back = lax.ppermute(inner, "col", swap("col", 1))
    done = (inner,)
    (back,) = call(hold_kernel, [backs[3]], [shape(backs[3].shape, BF16)], after=(inner,))
    backs[3] = lax.ppermute(back, ("grp", "col"), partners(3))
    done = physics(2, done)
    done = physics(1, done)
    for k in range(4, owners):
        done = physics(k, done)

    parts = lax.axis_size("row") * lax.axis_size("col")
    block = 2 * feats // parts
    if lax.axis_size("row") == 4 and lax.axis_size("col") == 2:
        keep, send = call(
            functools.partial(grads_kernel, owners),
            [*got, *acts, *dpres],
            [shape((2, 2, block, hidden), F32), shape((2, 2, block, hidden), BF16)],
        )
        arrived = lax.ppermute(send, "col", swap("col", 1))
        (gap,) = call(gap_kernel, [], [shape((8, 128), F32)], after=(keep,), flops=10000000000)
        mine, *shares = call(
            share_kernel,
            [keep, arrived],
            [shape((block, hidden), F32)] + [shape((block, hidden), BF16)] * 3,
            after=(gap,),
        )
        done = (mine,)
        shares = [lax.ppermute(s, "row", swap("row", bit)) for bit, s in zip((3, 1, 2), shares)]
        (summed,) = call(
            gather_kernel, [mine, *shares], [shape((block * hidden // 128, 128), F32)]
        )
    else:
        (flat,) = call(
            functools.partial(whole_grads_kernel, owners),
            [*got, *acts, *dpres],
            [shape((2 * feats, hidden), F32)],
        )
        done = (flat,)
        summed = lax.psum_scatter(
            flat.reshape(-1, 128), ("row", "col"), scatter_dimension=0, tiled=True
        )
    field, places = call(
        functools.partial(flow_kernel, wide, high),
        [flat_state, rate_col, near, far, inner_back, outer_back, place_row],
        [shape((count, feats), F32), shape((count, owners * cap), BF16)],
        [
            pltpu.VMEM((2, high + 2 * STEPS, wide + 2 * STEPS, feats), F32),
            pltpu.VMEM((high + 2 * STEPS, wide + 2 * STEPS, 128), F32),
        ],
        after=done,
    )
    new_state, column_adjoint = call(
        functools.partial(finish_kernel, owners),
        [field, places, *backs],
        [shape((count, feats), F32), shape((count, feats), BF16)],
    )
    return (
        new_state.reshape(state.shape),
        column_adjoint.reshape(state.shape),
        summed[None],
    )


def solution(mesh):
    in_specs = (
        P("row", ("grp", "col"), None),
        P("row", ("grp", "col")),
        P("row", ("grp", "col"), None),
        P("row", ("grp", "col"), None, None),
        P("grp", None, None),
        P("grp", None, None),
    )
    out_specs = (
        P("row", ("grp", "col"), None),
        P("row", ("grp", "col"), None),
        P("grp", ("row", "col"), None),
    )
    return jax.shard_map(local, mesh=mesh, in_specs=in_specs, out_specs=out_specs, check_vma=False)
```
